32 devices in a mesh: wave: 16 (over z, y, x), lev: 2 (over core).
Axes of the slice: x: 2, y: 2, z: 4, core: 2. Of those that a mesh axis runs over, the one named last changes fastest.
Arguments:
- spectra: bfloat16 [2, 3, 2, 1280, 1280], P('lev', None, None, None, 'wave'), may hold values from -0.119628906 to 0.119628906
- legendre: bfloat16 [1280, 16, 1280], P('wave'), may hold values from -0.15625 to 0.15625
- slot_wavenumbers: int32 [1280], replicated, may hold values from 0 to 1279, each once
- cycle_points: int32 [16], P('wave'), may hold values from 20 to 5136, as said below
- layer_depth_scaling: float32 [2], P('lev'), may hold values from 0.1 to 1
Outputs:
- physical_space_values: float32 [2, 16, 2, 3, 5376], P(None, 'wave', 'lev')
- height_potential_energy: float32 [2, 16, 2, 5376], P(None, 'wave', 'lev')
The draws below stay inside these ranges and needn't reach their ends.
Inputs may be any that keep to these rules, and one draw needn't show every extreme that they name: `slot_wavenumbers`: each wavenumber stands in exactly one slot. `cycle_points`: each entry is 20 + 4 i for a latitude index i of 0 to 1279 counted from the pole; some entry has i = 1279.
All inputs are finite; a program needn't handle non-finite values.
Results may differ from the reference program's by a relative error of at most 0.0037.
Values may be sent and summed in bfloat16 or wider, within the bound.
No kernel may reach another device: no remote copies, remote signals or barrier semaphores. Data moves between devices by JAX's collectives and lax.ppermute only.
A program may use at most 128 MiB of HBM per device.

```python
import math
import jax
import jax.numpy as jnp
from jax import lax

MW = 1280
FIELDS = 3
LEVELS = 2
NLATH = 16
PCOL = 5376


def draw_cycle_points(key, part):
    latitude = jax.random.randint(key, (NLATH,), 0, MW)
    widest = jax.random.randint(jax.random.fold_in(key, 7), (), 0, NLATH)
    latitude = jnp.where(jnp.arange(NLATH, dtype=jnp.int32) == widest, MW - 1, latitude)
    return (20 + 4 * latitude).astype(jnp.int32)


def levels(rng, extent, cuts, least, largest):
    gain = 1.0
    for position, shards_of in cuts:
        steps = jax.random.uniform(jax.random.fold_in(jax.random.fold_in(rng, 6), position), (shards_of,), jnp.float32, least / len(cuts), largest / len(cuts))
        gain = gain * jnp.repeat(jnp.exp(steps), extent[position] // shards_of).reshape((-1,) + (1,) * (len(extent) - 1 - position))
    return gain


def gaussian(rng, extent, scale, bound, cuts=(), kind=jnp.bfloat16):
    result = jax.random.normal(rng, extent, jnp.float32) * scale
    if len(cuts) > 0:
        result = levels(rng, extent, cuts, -0.22, 0.18) * result
    return jnp.clip(result, min=-bound, max=bound).astype(kind)


def setup_inputs(seed: int = 0) -> dict:
    keys = jax.random.split(jax.random.key(seed), 6)
    return {
        "spectra": gaussian(keys[0], (LEVELS, FIELDS, 2, MW, MW), 0.02, 0.119628906, ((0, 2), (4, 16))),
        "legendre": gaussian(keys[1], (MW, NLATH, MW), MW ** -0.5, 0.15625, ((0, 16),)),
        "slot_wavenumbers": jax.random.permutation(keys[2], MW).astype(jnp.int32),
        "cycle_points": draw_cycle_points(jax.random.fold_in(keys[5], 71), 0),
        "layer_depth_scaling": jnp.clip(jnp.exp(math.log(1.0) - 2.3025851 * jax.random.uniform(keys[4], (LEVELS,), jnp.float32) ** levels(keys[4], (LEVELS,), ((0, 2),), -0.2, 0.2)), 0.1, 1.0),
    }


full_turn = 2.0 * math.pi


def synth_table(wavenumber, points, offset, width):
    sample = offset + jnp.arange(width, dtype=jnp.int32)
    residue = (wavenumber[:, None] * sample[None, :]) % points
    angle = residue.astype(jnp.float32) * (full_turn / points.astype(jnp.float32))
    gaussian_integration_share = jnp.where(wavenumber == 0, 1.0, 2.0).astype(jnp.float32)[:, None]
    present = sample[None, :] < points
    cosine = jnp.where(present, gaussian_integration_share * jnp.cos(angle), 0.0)
    sine_rows = jnp.where(present, -gaussian_integration_share * jnp.sin(angle), 0.0)
    return jnp.concatenate([cosine, sine_rows], 0).astype(jnp.bfloat16)


def reference(spectra, legendre, slot_wavenumbers, cycle_points, layer_depth_scaling):
    columns_count = LEVELS * FIELDS * 2
    columns = jnp.transpose(spectra.reshape(columns_count, MW, MW), (1, 0, 2))
    degree = jnp.arange(MW, dtype=jnp.int32)

    def one_slot(input_arrays):
        basis, spectrum, wavenumber = input_arrays
        present = degree >= wavenumber
        even_mask = present & ((degree + wavenumber) % 2 == 0)
        odd_mask = present & ((degree + wavenumber) % 2 == 1)
        blank = jnp.zeros_like(spectrum)
        even_spec = jnp.where(even_mask[None, :], spectrum, blank)
        odd_spec = jnp.where(odd_mask[None, :], spectrum, blank)
        basis_wide = basis.astype(jnp.float32)
        even_part = jnp.dot(basis_wide, even_spec.astype(jnp.float32).T, preferred_element_type=jnp.float32)
        odd_part = jnp.dot(basis_wide, odd_spec.astype(jnp.float32).T, preferred_element_type=jnp.float32)
        return jnp.stack([even_part + odd_part, even_part - odd_part], 0).astype(jnp.bfloat16)

    fourier = lax.map(one_slot, (legendre, columns, slot_wavenumbers))

    def single_latitude_line(input_arrays):
        rows, points = input_arrays
        matrix = jnp.transpose(rows, (1, 2, 0)).reshape(2 * LEVELS * FIELDS, 2 * MW)
        basis = synth_table(slot_wavenumbers, points, 0, PCOL)
        values = jnp.dot(matrix.astype(jnp.float32), basis.astype(jnp.float32), preferred_element_type=jnp.float32)
        return values.reshape(2, LEVELS, FIELDS, PCOL)

    physical_space_values = lax.map(single_latitude_line, (jnp.transpose(fourier, (2, 0, 1, 3)), cycle_points))
    physical_space_values = jnp.transpose(physical_space_values, (1, 0, 2, 3, 4))
    thermal_state_values = physical_space_values[:, :, :, 0, :] * layer_depth_scaling[None, None, :, None]
    height_potential_energy = jnp.flip(jnp.cumsum(jnp.flip(thermal_state_values, 2), axis=2), 2)
    return physical_space_values, height_potential_energy
```

```python
import functools
import math

import jax
import jax.numpy as jnp
from jax import lax
from jax.experimental import pallas as pl
from jax.experimental.pallas import tpu as pltpu
from jax.sharding import PartitionSpec as P

PCOL = 5376
LANES = 128
FINE = 256
COARSE = PCOL // FINE
GROUP = 16
WIDE = 64
REST = 16
VMEM = 56 * 1024 * 1024


def cost(flops, size):
    return pl.CostEstimate(flops=flops, bytes_accessed=size, transcendentals=0)


def params():
    return pltpu.CompilerParams(vmem_limit_bytes=VMEM)


def block_rows(columns, slots):
    groups = columns * slots // GROUP
    return (groups // 2 + -(-groups // 8)) * GROUP


def pack_kernel(x_ref, o_ref):
    columns, _, rows = x_ref.shape
    targets = o_ref.shape[0]
    slots = rows // targets
    parts = slots // GROUP
    groups = columns * parts
    turned = [jnp.transpose(x_ref[c]) for c in range(columns)]
    for t in range(targets):
        base = t * slots
        for f in range(columns // 2):
            real = turned[2 * f][base : base + slots, :WIDE]
            imag = turned[2 * f + 1][base : base + slots, :WIDE]
            o_ref[t, f * slots : (f + 1) * slots, :] = jnp.concatenate([real, imag], 1)
        start = columns // 2 * slots
        for r in range(-(-groups // 8)):
            pieces = []
            for k in range(8):
                q = min(8 * r + k, groups - 1)
                c, s = q // parts, base + q % parts * GROUP
                pieces.append(turned[c][s : s + GROUP, WIDE:])
            o_ref[t, start + r * GROUP : start + (r + 1) * GROUP, :] = jnp.concatenate(pieces, 1)


def pack(x, targets):
    columns, degrees, rows = x.shape
    out_rows = block_rows(columns, rows // targets)
    return pl.pallas_call(
        pack_kernel,
        in_specs=[pl.BlockSpec(memory_space=pltpu.VMEM)],
        out_specs=pl.BlockSpec(memory_space=pltpu.VMEM),
        out_shape=jax.ShapeDtypeStruct((targets, out_rows, LANES), x.dtype),
        compiler_params=params(),
        cost_estimate=cost(0, 4_000_000),
        name="pack",
    )(x)


def basis_kernel(x_ref, m_ref, o_ref):
    group, lats, degrees = x_ref.shape
    width = group * lats
    x = x_ref[...].reshape(width, degrees)
    row = lax.broadcasted_iota(jnp.int32, (width, width), 0)
    column = lax.broadcasted_iota(jnp.int32, (width, width), 1)
    move = (row == column % group * lats + column // group).astype(jnp.float32).astype(x.dtype)
    turned = lax.dot_general(x, move, (((0,), (0,)), ((), ())), preferred_element_type=jnp.float32)
    degree = lax.broadcasted_iota(jnp.int32, (degrees, width), 0)
    live = jnp.where(degree >= m_ref[0], turned, 0.0).astype(o_ref.dtype)
    span = WIDE + REST
    sources = degrees // span
    for e in range(sources):
        o_ref[0, e * WIDE : (e + 1) * WIDE, :] = live[e * span : e * span + WIDE, :]
        to = sources * WIDE + e * REST
        o_ref[0, to : to + REST, :] = live[e * span + WIDE : (e + 1) * span, :]


def basis(legendre, waves):
    slots, lats, degrees = legendre.shape
    parts = slots // GROUP
    width = GROUP * lats
    return pl.pallas_call(
        basis_kernel,
        grid=(parts,),
        in_specs=[
            pl.BlockSpec((GROUP, lats, degrees), lambda i: (i, 0, 0)),
            pl.BlockSpec((1, 1, width), lambda i: (i, 0, 0)),
        ],
        out_specs=pl.BlockSpec((1, degrees, width), lambda i: (i, 0, 0)),
        out_shape=jax.ShapeDtypeStruct((parts, degrees, width), legendre.dtype),
        compiler_params=params(),
        cost_estimate=cost(2 * slots * lats * degrees * 256, 7_000_000),
        name="basis",
    )(legendre, waves)


def section_kernel(copies, r_ref, b_ref, m_ref, _, scale_ref, o_ref, s_ref):
    sources = r_ref.shape[0]
    parts, degrees, width = b_ref.shape
    lats = width // GROUP
    columns = s_ref.shape[0] // (2 * GROUP)
    slots = parts * GROUP
    half = columns * GROUP
    start = columns // 2 * slots
    sign = 1.0 - 2.0 * (lax.broadcasted_iota(jnp.int32, (half, degrees), 1) % 2).astype(jnp.float32)
    sign = sign.astype(s_ref.dtype)
    row = lax.broadcasted_iota(jnp.int32, (2 * half, width), 0)
    lane = lax.broadcasted_iota(jnp.int32, (2 * half, width), 1)
    same = row % GROUP == lane % GROUP
    fields = columns // 2
    pick_row = lax.broadcasted_iota(jnp.int32, (16, 2 * half), 0)
    pick_lane = lax.broadcasted_iota(jnp.int32, (16, 2 * half), 1)
    part, place = pick_row // 8, pick_row % 8
    spare = place >= 2 * fields
    hemisphere = jnp.where(spare, place - 2 * fields, place // fields)
    field = jnp.where(spare, 0, place % fields)
    pick = pick_lane // GROUP == hemisphere * columns + field * 2 + part
    pick = pick.astype(jnp.float32).astype(s_ref.dtype)
    out_row = lax.broadcasted_iota(jnp.int32, (16, width), 0) % 8
    south = ((out_row >= fields) & (out_row < 2 * fields)) | (out_row == 2 * fields + 1)
    rows = []
    for g in range(parts):
        for c in range(columns):
            at = c // 2 * slots + g * GROUP
            lo = c % 2 * WIDE
            q = c * parts + g
            rest_at, rest_lo = start + q // 8 * GROUP, q % 8 * REST
            to = slice(c * GROUP, (c + 1) * GROUP)
            wide = [r_ref[e, at : at + GROUP, lo : lo + WIDE] for e in range(sources)]
            rest = [r_ref[e, rest_at : rest_at + GROUP, rest_lo : rest_lo + REST] for e in range(sources)]
            s_ref[to, :] = jnp.concatenate(wide + rest, 1)
        s_ref[half:, :] = s_ref[:half, :] * sign
        sums = jnp.dot(s_ref[...], b_ref[g], preferred_element_type=jnp.float32)
        own = jnp.where(same, sums, 0.0).astype(s_ref.dtype)
        found = jnp.dot(pick, own, preferred_element_type=jnp.float32)
        parity = (1 - 2 * (m_ref[g] % 2)).astype(jnp.float32)
        rows.append(jnp.where(south, found * parity, found))
    blank = jnp.zeros((16, LANES - slots), jnp.float32)
    for l in range(lats):
        pieces = [r[:, l * GROUP : (l + 1) * GROUP] for r in rows] + [blank]
        tile = jnp.concatenate(pieces, 1).astype(o_ref.dtype)
        for v in range(copies):
            o_ref[l, v] = tile


def section(received, table, waves, ready, scales, columns, copies):
    parts, degrees, width = table.shape
    lats = width // GROUP
    return pl.pallas_call(
        functools.partial(section_kernel, copies),
        in_specs=[pl.BlockSpec(memory_space=pltpu.VMEM)] * 3
        + [pl.BlockSpec(memory_space=pl.ANY), pl.BlockSpec(memory_space=pltpu.SMEM)],
        out_specs=pl.BlockSpec(memory_space=pltpu.VMEM),
        out_shape=jax.ShapeDtypeStruct((lats, copies, 16, LANES), received.dtype),
        scratch_shapes=[pltpu.VMEM((2 * columns * GROUP, degrees), received.dtype)],
        compiler_params=params(),
        cost_estimate=cost(10_000_000_000, 4_000_000),
        name="section",
    )(received, table, waves, ready, scales)


def plain_section(received, legendre, waves, copies):
    columns, slots, degrees = received.shape
    fields = columns // 2
    degree = lax.broadcasted_iota(jnp.int32, (slots, degrees), 1)
    live = degree >= waves[:, None]
    odd = (degree + waves[:, None]) % 2 == 1
    blank = jnp.zeros_like(received)
    north = jnp.where(live[None], received, blank)
    south = jnp.where(odd[None], -north, north)
    both = jnp.stack([north, south], 0).reshape(2, fields, 2, slots, degrees)
    sums = jnp.einsum("sln,hfisn->lihfs", legendre, both, preferred_element_type=jnp.float32)
    lats = legendre.shape[1]
    rows = jnp.concatenate([sums.reshape(lats, 2, 2 * fields, slots), sums[:, :, :, 0]], 2)
    rows = rows.reshape(lats, 16, slots).astype(received.dtype)
    rows = jnp.pad(rows, ((0, 0), (0, 0), (0, LANES - slots)))
    return jnp.broadcast_to(rows[:, None], (lats, copies, 16, LANES))


def turn(product, points):
    inverse = 1.0 / points
    whole = jnp.floor(product * inverse + 0.5)
    residue = product - whole * points
    quarter = jnp.floor(4.0 * residue * inverse + 0.5)
    small = (4.0 * residue - quarter * points) * inverse * (0.5 * math.pi)
    square = small * small
    sine = small * (1.0 + square * (-1.0 / 6 + square * (1.0 / 120 + square * (-1.0 / 5040))))
    cosine = 1.0 + square * (-0.5 + square * (1.0 / 24 + square * (-1.0 / 720 + square * (1.0 / 40320))))
    which = quarter.astype(jnp.int32) & 3
    swap = (which & 1) == 1
    first = jnp.where(swap, sine, cosine)
    second = jnp.where(swap, cosine, sine)
    first = jnp.where((which == 1) | (which == 2), -first, first)
    second = jnp.where(which >= 2, -second, second)
    return first, second


def table_kernel(points_ref, m_ref, t_ref, c_ref, s_ref):
    points = points_ref[0].astype(jnp.float32)
    m = m_ref[0].astype(jnp.float32)
    down = jnp.transpose(jnp.broadcast_to(m, (LANES, LANES)))
    down = jnp.concatenate([down] * (FINE // LANES), 1)
    point = lax.broadcasted_iota(jnp.int32, (LANES, FINE), 1).astype(jnp.float32)
    cosine, sine = turn(down * point, points)
    t_ref[0] = cosine.astype(t_ref.dtype)
    t_ref[1] = (-sine).astype(t_ref.dtype)
    coarse = lax.broadcasted_iota(jnp.int32, c_ref.shape, 0) * FINE
    cosine, sine = turn(m * coarse.astype(jnp.float32), points)
    share = jnp.where(m == 0.0, 1.0, 2.0)
    c_ref[...] = cosine * share
    s_ref[...] = sine * share


def tables(points, slot_waves):
    sources = slot_waves.shape[0]
    depth = sources * LANES
    steps = -(-COARSE // 8) * 8
    return pl.pallas_call(
        table_kernel,
        grid=(sources,),
        in_specs=[
            pl.BlockSpec(memory_space=pltpu.SMEM),
            pl.BlockSpec((1, 1, LANES), lambda i: (i, 0, 0)),
        ],
        out_specs=[
            pl.BlockSpec((2, LANES, FINE), lambda i: (0, i, 0)),
            pl.BlockSpec((steps, LANES), lambda i: (0, i)),
            pl.BlockSpec((steps, LANES), lambda i: (0, i)),
        ],
        out_shape=[
            jax.ShapeDtypeStruct((2, depth, FINE), jnp.bfloat16),
            jax.ShapeDtypeStruct((steps, depth), jnp.float32),
            jax.ShapeDtypeStruct((steps, depth), jnp.float32),
        ],
        compiler_params=params(),
        cost_estimate=cost(60_000_000, 3_000_000),
        name="tables",
    )(points, slot_waves)


def synth_kernel(points_ref, place_ref, scale_ref, r_ref, t_ref, c_ref, s_ref, v_ref, h_ref, g_ref):
    sources, levels = r_ref.shape[:2]
    depth = sources * LANES
    me = place_ref[0]
    fields = v_ref.shape[1]
    row = lax.broadcasted_iota(jnp.int32, (16, LANES), 0) % 8
    spare = row >= 2 * fields
    weights = []
    for v in range(levels):
        summed = jnp.where(v >= me, scale_ref[v], 0.0)
        single = jnp.where(v == me, 1.0, 0.0)
        weights.append(jnp.where(spare, summed, single))

    def fill(e, carry):
        rows = sum(weights[v] * r_ref[e, v].astype(jnp.float32) for v in range(levels))
        real, imag = rows[:8], rows[8:]
        lanes = pl.ds(pl.multiple_of(e * LANES, LANES), LANES)
        shifted = pl.ds(pl.multiple_of(depth + e * LANES, LANES), LANES)
        for pair in range(g_ref.shape[0] // 16):
            first, second = [], []
            for b in (2 * pair, 2 * pair + 1):
                cosine, sine = c_ref[b : b + 1, lanes], s_ref[b : b + 1, lanes]
                first.append(real * cosine - imag * sine)
                second.append(real * sine + imag * cosine)
            to = slice(pair * 16, pair * 16 + 16)
            g_ref[to, lanes] = jnp.concatenate(first, 0).astype(g_ref.dtype)
            g_ref[to, shifted] = jnp.concatenate(second, 0).astype(g_ref.dtype)
        return carry

    lax.fori_loop(0, sources, fill, 0)
    table = t_ref[...].reshape(2 * depth, FINE)
    values = jnp.dot(g_ref[...], table, preferred_element_type=jnp.float32)
    lane = lax.broadcasted_iota(jnp.int32, (8, FINE), 1)
    for b in range(COARSE):
        at = slice(b * FINE, (b + 1) * FINE)
        part = jnp.where(lane + b * FINE < points_ref[0], values[8 * b : 8 * b + 8], 0.0)
        for h in range(2):
            for f in range(fields):
                v_ref[h, f, :, at] = part[h * fields + f : h * fields + f + 1]
            h_ref[h, 0, :, at] = part[2 * fields + h : 2 * fields + h + 1]


def synthesis(points, place, scales, received, table, cosine, sine, fields):
    depth = received.shape[0] * LANES
    smem, vmem = pl.BlockSpec(memory_space=pltpu.SMEM), pl.BlockSpec(memory_space=pltpu.VMEM)
    return pl.pallas_call(
        synth_kernel,
        in_specs=[smem] * 3 + [vmem] * 4,
        out_specs=[vmem] * 2,
        out_shape=[
            jax.ShapeDtypeStruct((2, fields, 1, PCOL), jnp.float32),
            jax.ShapeDtypeStruct((2, 1, 1, PCOL), jnp.float32),
        ],
        scratch_shapes=[pltpu.VMEM(((COARSE + 1) // 2 * 16, 2 * depth), jnp.bfloat16)],
        compiler_params=params(),
        cost_estimate=cost(1_000_000_000, 3_000_000),
        name="synth",
    )(points, place, scales, received, table, cosine, sine)


def shards(spectra, legendre, slot_wavenumbers, cycle_points, layer_depth_scaling):
    slots, lats, degrees = legendre.shape
    levels_here, fields = spectra.shape[:2]
    assert levels_here == 1 and cycle_points.shape[0] == 1 and fields == 3
    waves, levels = lax.axis_size("wave"), lax.axis_size("lev")
    columns = fields * 2
    own = lax.dynamic_slice_in_dim(slot_wavenumbers, lax.axis_index("wave") * slots, slots)
    x = spectra.reshape(columns, waves * slots, spectra.shape[4])
    slot_waves = jnp.pad(slot_wavenumbers.reshape(waves, slots), ((0, 0), (0, LANES - slots)))
    table, cosine, sine = tables(cycle_points, slot_waves.reshape(waves, 1, LANES))
    scales = lax.all_gather(layer_depth_scaling, "lev", tiled=True)
    place = lax.axis_index("lev").reshape(1)
    if spectra.shape[4] == WIDE + REST and slots % GROUP == 0 and lats == 16:
        parts = slots // GROUP
        spread = jnp.broadcast_to(own.reshape(parts, 1, GROUP), (parts, lats, GROUP))
        spread = spread.reshape(parts, 1, lats * GROUP)
        sent = pack(jnp.swapaxes(x, 1, 2), waves)
        received = lax.all_to_all(sent, "wave", 0, 0, tiled=True)
        rows = section(received, basis(legendre, spread), spread, cosine, scales, columns, levels)
    else:
        received = lax.all_to_all(x, "wave", split_axis=1, concat_axis=2, tiled=True)
        rows = plain_section(received, legendre, own, levels)
    rows = rows.reshape(waves * levels, 16, LANES)
    rows = lax.all_to_all(rows, ("wave", "lev"), 0, 0, tiled=True)
    rows = rows.reshape(waves, levels, 16, LANES)
    values, height = synthesis(cycle_points, place, scales, rows, table, cosine, sine, fields)
    return jnp.transpose(values, (0, 2, 1, 3))[:, :, None], height


def solution(mesh):
    in_specs = (P("lev", None, None, None, "wave"), P("wave", None, None), P(), P("wave"), P("lev"))
    out_specs = (P(None, "wave", "lev", None, None), P(None, "wave", "lev", None))
    call = jax.shard_map(shards, mesh=mesh, in_specs=in_specs, out_specs=out_specs, check_vma=False)

    def whole(*arrays):
        values, height = call(*arrays)
        return values, height

    return whole
```

```python
import functools
import math

import jax
import jax.numpy as jnp
from jax import lax
from jax.experimental import pallas as pl
from jax.experimental.pallas import tpu as pltpu
from jax.sharding import PartitionSpec as P

PCOL = 5376
LANES = 128
FINE = 256
COARSE = PCOL // FINE
GROUP = 16
WIDE = 64
REST = 16


def cost(flops, size):
    return pl.CostEstimate(flops=flops, bytes_accessed=size, transcendentals=0)


def params(size=16):
    return pltpu.CompilerParams(vmem_limit_bytes=size * 1024 * 1024)


def block_rows(columns, slots):
    groups = columns * slots // GROUP
    return (groups // 2 + -(-groups // 8)) * GROUP


def pack_kernel(x_hbm, o_hbm, x_ref, o_ref, in_sems, out_sems):
    columns, _, rows = x_ref.shape
    targets = o_ref.shape[0]
    slots = rows // targets
    parts = slots // GROUP
    groups = columns * parts
    loads, stores = [], []
    for i in range(2):
        some = pl.ds(i * columns // 2, columns // 2)
        loads.append(pltpu.make_async_copy(x_hbm.at[some], x_ref.at[some], in_sems.at[i]))
        loads[i].start()
    turned = []
    for c in range(columns):
        if c % (columns // 2) == 0:
            loads[c // (columns // 2)].wait()
        turned.append(jnp.transpose(x_ref[c]))
    chunk = targets // 4
    for t in range(targets):
        base = t * slots
        for g in range(parts):
            s = slice(base + g * GROUP, base + (g + 1) * GROUP)
            for f in range(columns // 2):
                at = (g * columns // 2 + f) * GROUP
                real, imag = turned[2 * f][s, :WIDE], turned[2 * f + 1][s, :WIDE]
                o_ref[t, at : at + GROUP, :] = jnp.concatenate([real, imag], 1)
        start = columns // 2 * slots
        for r in range(-(-groups // 8)):
            pieces = []
            for k in range(8):
                q = min(8 * r + k, groups - 1)
                s = base + q // columns * GROUP
                pieces.append(turned[q % columns][s : s + GROUP, WIDE:])
            o_ref[t, start + r * GROUP : start + (r + 1) * GROUP, :] = jnp.concatenate(pieces, 1)
        if (t + 1) % chunk == 0:
            i = t // chunk
            some = pl.ds(i * chunk, chunk)
            stores.append(pltpu.make_async_copy(o_ref.at[some], o_hbm.at[some], out_sems.at[i]))
            stores[i].start()
    for store in stores:
        store.wait()


def pack(x, targets):
    columns, degrees, rows = x.shape
    out = (targets, block_rows(columns, rows // targets), LANES)
    return pl.pallas_call(
        pack_kernel,
        in_specs=[pl.BlockSpec(memory_space=pl.ANY)],
        out_specs=pl.BlockSpec(memory_space=pl.ANY),
        out_shape=jax.ShapeDtypeStruct(out, x.dtype),
        scratch_shapes=[
            pltpu.VMEM(x.shape, x.dtype),
            pltpu.VMEM(out, x.dtype),
            pltpu.SemaphoreType.DMA((2,)),
            pltpu.SemaphoreType.DMA((4,)),
        ],
        compiler_params=params(56),
        cost_estimate=cost(0, 4_000_000),
        name="pack",
    )(x)


def section_kernel(copies, r_hbm, x_ref, m_ref, *rest):
    o_ref, r_ref, s_ref, f_ref, sem = rest[-5:]
    sources = r_ref.shape[0]
    slots, lats, degrees = x_ref.shape
    parts = slots // GROUP
    width = GROUP * lats
    columns = s_ref.shape[1] // (2 * GROUP)
    fields = columns // 2
    half = columns * GROUP
    start = columns // 2 * slots
    arrive = pltpu.make_async_copy(r_hbm, r_ref, sem)
    arrive.start()
    row = lax.broadcasted_iota(jnp.int32, (2 * half, width), 0)
    lane = lax.broadcasted_iota(jnp.int32, (2 * half, width), 1)
    same = (row % GROUP == lane // lats).reshape(2 * columns, GROUP, width)
    degree = lax.broadcasted_iota(jnp.int32, (GROUP, degrees), 1)
    arrive.wait()
    for g in range(parts):
        wave = m_ref[g * GROUP : (g + 1) * GROUP, :]
        live = degree >= wave
        sign = (1 - 2 * ((degree + wave) % 2)).astype(jnp.float32)
        north = jnp.where(live, 1.0, 0.0).astype(s_ref.dtype)
        south = jnp.where(live, sign, 0.0).astype(s_ref.dtype)
        for c in range(columns):
            at = (g * columns // 2 + c // 2) * GROUP
            lo = c % 2 * WIDE
            q = g * columns + c
            rest_at, rest_lo = start + q // 8 * GROUP, q % 8 * REST
            pieces = []
            for e in range(sources):
                pieces.append(r_ref[e, at : at + GROUP, lo : lo + WIDE])
                pieces.append(r_ref[e, rest_at : rest_at + GROUP, rest_lo : rest_lo + REST])
            tile = jnp.concatenate(pieces, 1)
            to = (c % 2 * 2 * fields + c // 2) * GROUP
            s_ref[g, to : to + GROUP, :] = tile * north
            to += fields * GROUP
            s_ref[g, to : to + GROUP, :] = tile * south
        basis = x_ref[g * GROUP : (g + 1) * GROUP].reshape(width, degrees)
        sums = lax.dot_general(
            s_ref[g], basis, (((1,), (1,)), ((), ())), preferred_element_type=jnp.float32
        )
        found = jnp.sum(jnp.where(same, sums.reshape(same.shape), 0.0), axis=1)
        for i in range(2):
            at, first = g * 16 + 8 * i, 2 * fields * i
            f_ref[at : at + 2 * fields, :] = found[first : first + 2 * fields]
            f_ref[at + 2 * fields : at + 2 * fields + 1, :] = found[first : first + 1]
            f_ref[at + 2 * fields + 1 : at + 8, :] = found[first + fields : first + fields + 1]
    source = lax.broadcasted_iota(jnp.int32, (width, width), 0)
    target = lax.broadcasted_iota(jnp.int32, (width, width), 1)
    move = (target == source % lats * GROUP + source // lats).astype(jnp.float32).astype(s_ref.dtype)
    moved = jnp.dot(f_ref[...].astype(s_ref.dtype), move, preferred_element_type=jnp.float32)
    blank = jnp.zeros((16, LANES - slots), jnp.float32)
    for l in range(lats):
        pieces = [moved[g * 16 : (g + 1) * 16, l * GROUP : (l + 1) * GROUP] for g in range(parts)]
        tile = jnp.concatenate(pieces + [blank], 1).astype(o_ref.dtype)
        for v in range(copies):
            o_ref[l, v] = tile


def section(received, legendre, waves, ready, columns, copies):
    slots, lats, degrees = legendre.shape
    parts = slots // GROUP
    spaces = [pl.ANY, pltpu.VMEM, pltpu.VMEM] + [pl.ANY] * len(ready)
    return pl.pallas_call(
        functools.partial(section_kernel, copies),
        in_specs=[pl.BlockSpec(memory_space=space) for space in spaces],
        out_specs=pl.BlockSpec(memory_space=pltpu.VMEM),
        out_shape=jax.ShapeDtypeStruct((lats, copies, 16, LANES), received.dtype),
        scratch_shapes=[
            pltpu.VMEM(received.shape, received.dtype),
            pltpu.VMEM((parts, 2 * columns * GROUP, degrees), received.dtype),
            pltpu.VMEM((parts * 16, GROUP * lats), jnp.float32),
            pltpu.SemaphoreType.DMA,
        ],
        compiler_params=params(),
        cost_estimate=cost(10_000_000_000, 4_000_000),
        name="section",
    )(received, legendre, waves, *ready)


def plain_section(received, legendre, waves, copies):
    columns, slots, degrees = received.shape
    fields = columns // 2
    degree = lax.broadcasted_iota(jnp.int32, (slots, degrees), 1)
    live = degree >= waves[:, None]
    odd = (degree + waves[:, None]) % 2 == 1
    blank = jnp.zeros_like(received)
    north = jnp.where(live[None], received, blank)
    south = jnp.where(odd[None], -north, north)
    both = jnp.stack([north, south], 0).reshape(2, fields, 2, slots, degrees)
    sums = jnp.einsum("sln,hfisn->lihfs", legendre, both, preferred_element_type=jnp.float32)
    lats = legendre.shape[1]
    rows = jnp.concatenate([sums.reshape(lats, 2, 2 * fields, slots), sums[:, :, :, 0]], 2)
    rows = rows.reshape(lats, 16, slots).astype(received.dtype)
    rows = jnp.pad(rows, ((0, 0), (0, 0), (0, LANES - slots)))
    return jnp.broadcast_to(rows[:, None], (lats, copies, 16, LANES))


def turn(product, points):
    inverse = 1.0 / points
    whole = jnp.floor(product * inverse + 0.5)
    residue = product - whole * points
    quarter = jnp.floor(4.0 * residue * inverse + 0.5)
    small = (4.0 * residue - quarter * points) * inverse * (0.5 * math.pi)
    square = small * small
    sine = small * (1.0 + square * (-1.0 / 6 + square * (1.0 / 120 + square * (-1.0 / 5040))))
    cosine = 1.0 + square * (-0.5 + square * (1.0 / 24 + square * (-1.0 / 720 + square * (1.0 / 40320))))
    which = quarter.astype(jnp.int32) & 3
    swap = (which & 1) == 1
    first = jnp.where(swap, sine, cosine)
    second = jnp.where(swap, cosine, sine)
    first = jnp.where((which == 1) | (which == 2), -first, first)
    second = jnp.where(which >= 2, -second, second)
    return first, second


def table_kernel(points_ref, m_ref, _, t_ref, c_ref, s_ref, done_ref):
    done_ref[...] = jnp.zeros_like(done_ref)
    points = points_ref[0].astype(jnp.float32)
    m = m_ref[...].astype(jnp.float32)
    down = jnp.transpose(jnp.broadcast_to(m, (LANES, LANES)))
    down = jnp.concatenate([down] * (FINE // LANES), 1)
    point = lax.broadcasted_iota(jnp.int32, (LANES, FINE), 1).astype(jnp.float32)
    cosine, sine = turn(down * point, points)
    t_ref[0] = cosine.astype(t_ref.dtype)
    t_ref[1] = (-sine).astype(t_ref.dtype)
    coarse = lax.broadcasted_iota(jnp.int32, c_ref.shape, 0) * FINE
    cosine, sine = turn(m * coarse.astype(jnp.float32), points)
    share = jnp.where(m == 0.0, 1.0, 2.0)
    c_ref[...] = cosine * share
    s_ref[...] = sine * share


def tables(points, slot_waves, early):
    depth = slot_waves.shape[1]
    steps = -(-COARSE // 8) * 8
    return pl.pallas_call(
        table_kernel,
        grid=(depth // LANES,),
        in_specs=[
            pl.BlockSpec(memory_space=pltpu.SMEM),
            pl.BlockSpec((1, LANES), lambda i: (0, i)),
            pl.BlockSpec(memory_space=pl.ANY),
        ],
        out_specs=[
            pl.BlockSpec((2, LANES, FINE), lambda i: (0, i, 0)),
            pl.BlockSpec((steps, LANES), lambda i: (0, i)),
            pl.BlockSpec((steps, LANES), lambda i: (0, i)),
            pl.BlockSpec((8, LANES), lambda i: (0, 0)),
        ],
        out_shape=[
            jax.ShapeDtypeStruct((2, depth, FINE), jnp.bfloat16),
            jax.ShapeDtypeStruct((steps, depth), jnp.float32),
            jax.ShapeDtypeStruct((steps, depth), jnp.float32),
            jax.ShapeDtypeStruct((8, LANES), jnp.float32),
        ],
        compiler_params=params(16),
        cost_estimate=cost(60_000_000, 3_000_000),
        name="tables",
    )(points, slot_waves, early)


def level_weights(scales, me, spare):
    level = jnp.arange(scales.shape[0])[:, None]
    row = jnp.arange(16)[None] % 8
    summed = jnp.where(level >= me, scales[:, None], 0.0)
    weights = jnp.where(row >= spare, summed, (level == me).astype(jnp.float32))
    return jnp.broadcast_to(weights[:, :, None], weights.shape + (LANES,))


def synth_kernel(points_ref, w_ref, r_ref, t_ref, c_ref, s_ref, v_ref, h_ref, g_ref):
    sources, levels = r_ref.shape[:2]
    depth = c_ref.shape[1]
    slots = depth // sources
    fields = v_ref.shape[1]
    pieces = []
    for e in range(sources):
        rows = sum(w_ref[v] * r_ref[e, v].astype(jnp.float32) for v in range(levels))
        pieces.append(rows[:, :slots])
    every = jnp.concatenate(pieces, 1)
    real, imag = every[:8], every[8:]
    for pair in range(g_ref.shape[0] // 16):
        first, second = [], []
        for b in (2 * pair, 2 * pair + 1):
            cosine, sine = c_ref[b : b + 1, :], s_ref[b : b + 1, :]
            first.append(real * cosine - imag * sine)
            second.append(real * sine + imag * cosine)
        to = slice(pair * 16, pair * 16 + 16)
        g_ref[to, :depth] = jnp.concatenate(first, 0).astype(g_ref.dtype)
        g_ref[to, depth:] = jnp.concatenate(second, 0).astype(g_ref.dtype)
    table = t_ref[...].reshape(2 * depth, FINE)
    values = jnp.dot(g_ref[...], table, preferred_element_type=jnp.float32)
    lane = lax.broadcasted_iota(jnp.int32, (8, FINE), 1)
    for b in range(COARSE):
        at = slice(b * FINE, (b + 1) * FINE)
        part = jnp.where(lane + b * FINE < points_ref[0], values[8 * b : 8 * b + 8], 0.0)
        for h in range(2):
            for f in range(fields):
                v_ref[h, f, :, at] = part[h * fields + f : h * fields + f + 1]
            h_ref[h, 0, :, at] = part[2 * fields + h : 2 * fields + h + 1]


def synthesis(points, weights, received, table, cosine, sine, fields):
    depth = cosine.shape[1]
    smem, vmem = pl.BlockSpec(memory_space=pltpu.SMEM), pl.BlockSpec(memory_space=pltpu.VMEM)
    return pl.pallas_call(
        synth_kernel,
        in_specs=[smem] + [vmem] * 5,
        out_specs=[vmem] * 2,
        out_shape=[
            jax.ShapeDtypeStruct((2, fields, 1, PCOL), jnp.float32),
            jax.ShapeDtypeStruct((2, 1, 1, PCOL), jnp.float32),
        ],
        scratch_shapes=[pltpu.VMEM(((COARSE + 1) // 2 * 16, 2 * depth), jnp.bfloat16)],
        compiler_params=params(),
        cost_estimate=cost(1_000_000_000, 3_000_000),
        name="synth",
    )(points, weights, received, table, cosine, sine)


def shards(spectra, legendre, slot_wavenumbers, cycle_points, layer_depth_scaling):
    slots, lats, degrees = legendre.shape
    levels_here, fields = spectra.shape[:2]
    assert levels_here == 1 and cycle_points.shape[0] == 1 and fields == 3
    waves, levels = lax.axis_size("wave"), lax.axis_size("lev")
    columns = fields * 2
    own = lax.dynamic_slice_in_dim(slot_wavenumbers, lax.axis_index("wave") * slots, slots)
    x = spectra.reshape(columns, waves * slots, spectra.shape[4])
    table, cosine, sine, done = tables(cycle_points, slot_wavenumbers[None], legendre)
    scales = lax.all_gather(layer_depth_scaling, "lev", tiled=True)
    weights = level_weights(scales, lax.axis_index("lev"), 2 * fields)
    if spectra.shape[4] == WIDE + REST and waves % 4 == 0 and fields == 3 and slots % GROUP == 0 and lats == 16:
        sent = pack(jnp.swapaxes(x, 1, 2), waves)
        received = lax.all_to_all(sent, "wave", 0, 0, tiled=True)
        ready = (done, weights)
        rows = section(received, legendre, own[:, None], ready, columns, levels)
    else:
        received = lax.all_to_all(x, "wave", split_axis=1, concat_axis=2, tiled=True)
        rows = plain_section(received, legendre, own, levels)
    rows = rows.reshape(waves * levels, 16, LANES)
    rows = lax.all_to_all(rows, ("wave", "lev"), 0, 0, tiled=True)
    rows = rows.reshape(waves, levels, 16, LANES)
    values, height = synthesis(cycle_points, weights, rows, table, cosine, sine, fields)
    return jnp.transpose(values, (0, 2, 1, 3))[:, :, None], height


def solution(mesh):
    in_specs = (P("lev", None, None, None, "wave"), P("wave", None, None), P(), P("wave"), P("lev"))
    out_specs = (P(None, "wave", "lev", None, None), P(None, "wave", "lev", None))
    call = jax.shard_map(shards, mesh=mesh, in_specs=in_specs, out_specs=out_specs, check_vma=False)

    def whole(*arrays):
        values, height = call(*arrays)
        return values, height

    return whole
```

```python
import functools
import math

import jax
import jax.numpy as jnp
from jax import lax
from jax.experimental import pallas as pl
from jax.experimental.pallas import tpu as pltpu
from jax.sharding import PartitionSpec as P

PCOL = 5376
LANES = 128
FINE = 256
COARSE = PCOL // FINE
GROUP = 16
WIDE = 64
REST = 16


def cost(flops, size):
    return pl.CostEstimate(flops=flops, bytes_accessed=size, transcendentals=0)


def params(size=16):
    return pltpu.CompilerParams(vmem_limit_bytes=size * 1024 * 1024)


def rest_place(c, g):
    return (g, c * REST) if g < 4 else (c // 2, (6 + c % 2) * REST)


def pack_kernel(x_hbm, o_hbm, x_ref, o_ref, in_sems, out_sems):
    columns, _, rows = x_ref.shape
    targets = o_ref.shape[0]
    slots = rows // targets
    fields = columns // 2
    loads, stores = [], []
    for f in range(fields):
        some = pl.ds(2 * f, 2)
        loads.append(pltpu.make_async_copy(x_hbm.at[some], x_ref.at[some], in_sems.at[f]))
        loads[f].start()
    wide = []
    for f in range(fields):
        loads[f].wait()
        both = jnp.concatenate([x_ref[2 * f, :WIDE, :], x_ref[2 * f + 1, :WIDE, :]], 0)
        wide.append(jnp.transpose(both))
    last = [x_ref[c, WIDE:, :] for c in range(columns)]
    rest = jnp.transpose(jnp.concatenate(last + last[:2], 0))
    chunk = targets // 4
    for t in range(targets):
        base = t * slots
        for f in range(fields):
            o_ref[t, f * slots : (f + 1) * slots, :] = wide[f][base : base + slots]
        groups = [rest[base + g * GROUP : base + (g + 1) * GROUP] for g in range(5)]
        for g in range(4):
            at = fields * slots + g * GROUP
            tile = groups[g]
            if g < fields:
                tile = jnp.concatenate([tile[:, : 6 * REST], groups[4][:, 2 * g * REST : 2 * (g + 1) * REST]], 1)
            o_ref[t, at : at + GROUP, :] = tile
        if (t + 1) % chunk == 0:
            i = t // chunk
            some = pl.ds(i * chunk, chunk)
            stores.append(pltpu.make_async_copy(o_ref.at[some], o_hbm.at[some], out_sems.at[i]))
            stores[i].start()
    for store in stores:
        store.wait()


def pack(x, targets):
    columns, degrees, rows = x.shape
    out = (targets, columns // 2 * (rows // targets) + 4 * GROUP, LANES)
    return pl.pallas_call(
        pack_kernel,
        in_specs=[pl.BlockSpec(memory_space=pl.ANY)],
        out_specs=pl.BlockSpec(memory_space=pl.ANY),
        out_shape=jax.ShapeDtypeStruct(out, x.dtype),
        scratch_shapes=[
            pltpu.VMEM(x.shape, x.dtype),
            pltpu.VMEM(out, x.dtype),
            pltpu.SemaphoreType.DMA((columns // 2,)),
            pltpu.SemaphoreType.DMA((4,)),
        ],
        compiler_params=params(56),
        cost_estimate=cost(0, 4_000_000),
        name="pack",
    )(x)


def section_kernel(copies, r_hbm, x_ref, m_ref, *rest):
    o_ref, r_ref, s_ref, f_ref, sem = rest[-5:]
    sources = r_ref.shape[0]
    slots, lats, degrees = x_ref.shape
    parts = slots // GROUP
    width = GROUP * lats
    columns = s_ref.shape[1] // (2 * GROUP)
    fields = columns // 2
    half = columns * GROUP
    arrive = pltpu.make_async_copy(r_hbm, r_ref, sem)
    arrive.start()
    row = lax.broadcasted_iota(jnp.int32, (2 * half, width), 0)
    lane = lax.broadcasted_iota(jnp.int32, (2 * half, width), 1)
    same = (row % GROUP == lane // lats).reshape(2 * columns, GROUP, width)
    degree = lax.broadcasted_iota(jnp.int32, (GROUP, degrees), 1)
    source = lax.broadcasted_iota(jnp.int32, (width, width), 0)
    target = lax.broadcasted_iota(jnp.int32, (width, width), 1)
    move = (target == source % lats * GROUP + source // lats).astype(jnp.float32).astype(s_ref.dtype)
    masks = []
    for g in range(parts):
        wave = m_ref[g * GROUP : (g + 1) * GROUP, :]
        live = degree >= wave
        sign = (1 - 2 * ((degree + wave) % 2)).astype(jnp.float32)
        north = jnp.where(live, 1.0, 0.0).astype(s_ref.dtype)
        south = jnp.where(live, sign, 0.0).astype(s_ref.dtype)
        masks.append((north, south))
    arrive.wait()
    for g in range(parts):
        north, south = masks[g]
        for c in range(columns):
            at = c // 2 * slots + g * GROUP
            lo = c % 2 * WIDE
            tile, rest_lo = rest_place(c, g)
            rest_at = fields * slots + tile * GROUP
            pieces = []
            for e in range(sources):
                pieces.append(r_ref[e, at : at + GROUP, lo : lo + WIDE])
                pieces.append(r_ref[e, rest_at : rest_at + GROUP, rest_lo : rest_lo + REST])
            tile = jnp.concatenate(pieces, 1)
            to = (c % 2 * 2 * fields + c // 2) * GROUP
            s_ref[g, to : to + GROUP, :] = tile * north
            to += fields * GROUP
            s_ref[g, to : to + GROUP, :] = tile * south
        basis = x_ref[g * GROUP : (g + 1) * GROUP].reshape(width, degrees)
        sums = lax.dot_general(
            s_ref[g], basis, (((1,), (1,)), ((), ())), preferred_element_type=jnp.float32
        )
        found = jnp.sum(jnp.where(same, sums.reshape(same.shape), 0.0), axis=1)
        for i in range(2):
            at, first = g * 16 + 8 * i, 2 * fields * i
            f_ref[at : at + 2 * fields, :] = found[first : first + 2 * fields]
            f_ref[at + 2 * fields : at + 2 * fields + 1, :] = found[first : first + 1]
            f_ref[at + 2 * fields + 1 : at + 8, :] = found[first + fields : first + fields + 1]
    moved = jnp.dot(f_ref[...].astype(s_ref.dtype), move, preferred_element_type=jnp.float32)
    blank = jnp.zeros((16, LANES - slots), jnp.float32)
    for l in range(lats):
        pieces = [moved[g * 16 : (g + 1) * 16, l * GROUP : (l + 1) * GROUP] for g in range(parts)]
        tile = jnp.concatenate(pieces + [blank], 1).astype(o_ref.dtype)
        for v in range(copies):
            o_ref[l, v] = tile


def section(received, legendre, waves, ready, columns, copies):
    slots, lats, degrees = legendre.shape
    parts = slots // GROUP
    spaces = [pl.ANY, pltpu.VMEM, pltpu.VMEM] + [pl.ANY] * len(ready)
    return pl.pallas_call(
        functools.partial(section_kernel, copies),
        in_specs=[pl.BlockSpec(memory_space=space) for space in spaces],
        out_specs=pl.BlockSpec(memory_space=pltpu.VMEM),
        out_shape=jax.ShapeDtypeStruct((lats, copies, 16, LANES), received.dtype),
        scratch_shapes=[
            pltpu.VMEM(received.shape, received.dtype),
            pltpu.VMEM((parts, 2 * columns * GROUP, degrees), received.dtype),
            pltpu.VMEM((parts * 16, GROUP * lats), jnp.float32),
            pltpu.SemaphoreType.DMA,
        ],
        compiler_params=params(),
        cost_estimate=cost(10_000_000_000, 4_000_000),
        name="section",
    )(received, legendre, waves, *ready)


def plain_section(received, legendre, waves, copies):
    columns, slots, degrees = received.shape
    fields = columns // 2
    degree = lax.broadcasted_iota(jnp.int32, (slots, degrees), 1)
    live = degree >= waves[:, None]
    odd = (degree + waves[:, None]) % 2 == 1
    blank = jnp.zeros_like(received)
    north = jnp.where(live[None], received, blank)
    south = jnp.where(odd[None], -north, north)
    both = jnp.stack([north, south], 0).reshape(2, fields, 2, slots, degrees)
    sums = jnp.einsum("sln,hfisn->lihfs", legendre, both, preferred_element_type=jnp.float32)
    lats = legendre.shape[1]
    rows = jnp.concatenate([sums.reshape(lats, 2, 2 * fields, slots), sums[:, :, :, 0]], 2)
    rows = rows.reshape(lats, 16, slots).astype(received.dtype)
    rows = jnp.pad(rows, ((0, 0), (0, 0), (0, LANES - slots)))
    return jnp.broadcast_to(rows[:, None], (lats, copies, 16, LANES))


def turn(product, points):
    inverse = 1.0 / points
    whole = jnp.floor(product * inverse + 0.5)
    residue = product - whole * points
    quarter = jnp.floor(4.0 * residue * inverse + 0.5)
    small = (4.0 * residue - quarter * points) * inverse * (0.5 * math.pi)
    square = small * small
    sine = small * (1.0 + square * (-1.0 / 6 + square * (1.0 / 120 + square * (-1.0 / 5040))))
    cosine = 1.0 + square * (-0.5 + square * (1.0 / 24 + square * (-1.0 / 720 + square * (1.0 / 40320))))
    which = quarter.astype(jnp.int32) & 3
    swap = (which & 1) == 1
    first = jnp.where(swap, sine, cosine)
    second = jnp.where(swap, cosine, sine)
    first = jnp.where((which == 1) | (which == 2), -first, first)
    second = jnp.where(which >= 2, -second, second)
    return first, second


def table_kernel(points_ref, m_ref, _, t_ref, c_ref, s_ref, done_ref):
    done_ref[...] = jnp.zeros_like(done_ref)
    points = points_ref[0].astype(jnp.float32)
    m = m_ref[...].astype(jnp.float32)
    down = jnp.transpose(jnp.broadcast_to(m, (LANES, LANES)))
    down = jnp.concatenate([down] * (FINE // LANES), 1)
    point = lax.broadcasted_iota(jnp.int32, (LANES, FINE), 1).astype(jnp.float32)
    cosine, sine = turn(down * point, points)
    t_ref[0] = cosine.astype(t_ref.dtype)
    t_ref[1] = (-sine).astype(t_ref.dtype)
    coarse = lax.broadcasted_iota(jnp.int32, c_ref.shape, 0) * FINE
    cosine, sine = turn(m * coarse.astype(jnp.float32), points)
    share = jnp.where(m == 0.0, 1.0, 2.0)
    c_ref[...] = cosine * share
    s_ref[...] = sine * share


def tables(points, slot_waves, early):
    depth = slot_waves.shape[1]
    steps = -(-COARSE // 8) * 8
    return pl.pallas_call(
        table_kernel,
        grid=(depth // LANES,),
        in_specs=[
            pl.BlockSpec(memory_space=pltpu.SMEM),
            pl.BlockSpec((1, LANES), lambda i: (0, i)),
            pl.BlockSpec(memory_space=pl.ANY),
        ],
        out_specs=[
            pl.BlockSpec((2, LANES, FINE), lambda i: (0, i, 0)),
            pl.BlockSpec((steps, LANES), lambda i: (0, i)),
            pl.BlockSpec((steps, LANES), lambda i: (0, i)),
            pl.BlockSpec((8, LANES), lambda i: (0, 0)),
        ],
        out_shape=[
            jax.ShapeDtypeStruct((2, depth, FINE), jnp.bfloat16),
            jax.ShapeDtypeStruct((steps, depth), jnp.float32),
            jax.ShapeDtypeStruct((steps, depth), jnp.float32),
            jax.ShapeDtypeStruct((8, LANES), jnp.float32),
        ],
        compiler_params=params(16),
        cost_estimate=cost(60_000_000, 3_000_000),
        name="tables",
    )(points, slot_waves, early)


def level_weights(scales, me, spare):
    level = jnp.arange(scales.shape[0])[:, None]
    row = jnp.arange(16)[None] % 8
    summed = jnp.where(level >= me, scales[:, None], 0.0)
    weights = jnp.where(row >= spare, summed, (level == me).astype(jnp.float32))
    return jnp.broadcast_to(weights[:, :, None], weights.shape + (LANES,))


def synth_kernel(points_ref, w_ref, r_ref, t_ref, c_ref, s_ref, v_ref, h_ref, g_ref):
    sources, levels = r_ref.shape[:2]
    depth = c_ref.shape[1]
    slots = depth // sources
    fields = v_ref.shape[1]
    pieces = []
    for e in range(sources):
        rows = sum(w_ref[v] * r_ref[e, v].astype(jnp.float32) for v in range(levels))
        pieces.append(rows[:, :slots])
    every = jnp.concatenate(pieces, 1)
    real, imag = every[:8], every[8:]
    for pair in range(g_ref.shape[0] // 16):
        first, second = [], []
        for b in (2 * pair, 2 * pair + 1):
            cosine, sine = c_ref[b : b + 1, :], s_ref[b : b + 1, :]
            first.append(real * cosine - imag * sine)
            second.append(real * sine + imag * cosine)
        to = slice(pair * 16, pair * 16 + 16)
        g_ref[to, :depth] = jnp.concatenate(first, 0).astype(g_ref.dtype)
        g_ref[to, depth:] = jnp.concatenate(second, 0).astype(g_ref.dtype)
    table = t_ref[...].reshape(2 * depth, FINE)
    values = jnp.dot(g_ref[...], table, preferred_element_type=jnp.float32)
    lane = lax.broadcasted_iota(jnp.int32, (8, FINE), 1)
    for b in range(COARSE):
        at = slice(b * FINE, (b + 1) * FINE)
        part = jnp.where(lane + b * FINE < points_ref[0], values[8 * b : 8 * b + 8], 0.0)
        for h in range(2):
            for f in range(fields):
                v_ref[h, f, :, at] = part[h * fields + f : h * fields + f + 1]
            h_ref[h, 0, :, at] = part[2 * fields + h : 2 * fields + h + 1]


def synthesis(points, weights, received, table, cosine, sine, fields):
    depth = cosine.shape[1]
    smem, vmem = pl.BlockSpec(memory_space=pltpu.SMEM), pl.BlockSpec(memory_space=pltpu.VMEM)
    return pl.pallas_call(
        synth_kernel,
        in_specs=[smem] + [vmem] * 5,
        out_specs=[vmem] * 2,
        out_shape=[
            jax.ShapeDtypeStruct((2, fields, 1, PCOL), jnp.float32),
            jax.ShapeDtypeStruct((2, 1, 1, PCOL), jnp.float32),
        ],
        scratch_shapes=[pltpu.VMEM(((COARSE + 1) // 2 * 16, 2 * depth), jnp.bfloat16)],
        compiler_params=params(),
        cost_estimate=cost(1_000_000_000, 3_000_000),
        name="synth",
    )(points, weights, received, table, cosine, sine)


def shards(spectra, legendre, slot_wavenumbers, cycle_points, layer_depth_scaling):
    slots, lats, degrees = legendre.shape
    levels_here, fields = spectra.shape[:2]
    assert levels_here == 1 and cycle_points.shape[0] == 1 and fields == 3
    waves, levels = lax.axis_size("wave"), lax.axis_size("lev")
    columns = fields * 2
    own = lax.dynamic_slice_in_dim(slot_wavenumbers, lax.axis_index("wave") * slots, slots)
    x = spectra.reshape(columns, waves * slots, spectra.shape[4])
    table, cosine, sine, done = tables(cycle_points, slot_wavenumbers[None], legendre)
    scales = lax.all_gather(layer_depth_scaling, "lev", tiled=True)
    weights = level_weights(scales, lax.axis_index("lev"), 2 * fields)
    if spectra.shape[4] == WIDE + REST and waves % 4 == 0 and fields == 3 and slots == 5 * GROUP and lats == 16:
        sent = pack(jnp.swapaxes(x, 1, 2), waves)
        received = lax.all_to_all(sent, "wave", 0, 0, tiled=True)
        ready = (done, weights)
        rows = section(received, legendre, own[:, None], ready, columns, levels)
    else:
        received = lax.all_to_all(x, "wave", split_axis=1, concat_axis=2, tiled=True)
        rows = plain_section(received, legendre, own, levels)
    rows = rows.reshape(waves * levels, 16, LANES)
    rows = lax.all_to_all(rows, ("wave", "lev"), 0, 0, tiled=True)
    rows = rows.reshape(waves, levels, 16, LANES)
    values, height = synthesis(cycle_points, weights, rows, table, cosine, sine, fields)
    return jnp.transpose(values, (0, 2, 1, 3))[:, :, None], height


def solution(mesh):
    in_specs = (P("lev", None, None, None, "wave"), P("wave", None, None), P(), P("wave"), P("lev"))
    out_specs = (P(None, "wave", "lev", None, None), P(None, "wave", "lev", None))
    call = jax.shard_map(shards, mesh=mesh, in_specs=in_specs, out_specs=out_specs, check_vma=False)

    def whole(*arrays):
        values, height = call(*arrays)
        return values, height

    return whole
```

```python
import functools
import math

import jax
import jax.numpy as jnp
from jax import lax
from jax.experimental import pallas as pl
from jax.experimental.pallas import tpu as pltpu
from jax.sharding import PartitionSpec as P

PCOL = 5376
LANES = 128
FINE = 256
COARSE = PCOL // FINE
GROUP = 16
WIDE = 64
REST = 16


def cost(flops, size):
    return pl.CostEstimate(flops=flops, bytes_accessed=size, transcendentals=0)


def params(size=16):
    return pltpu.CompilerParams(vmem_limit_bytes=size * 1024 * 1024)


def exchange_order(devices):
    bits = (devices - 1).bit_length()
    return sorted(range(devices), key=lambda i: int(format(i, "0" + str(bits) + "b")[::-1], 2))


def rest_place(c, g):
    return (g, c * REST) if g < 4 else (c // 2, (6 + c % 2) * REST)


def pack_kernel(x_hbm, o_hbm, x_ref, o_ref, in_sems, out_sems):
    columns, _, rows = x_ref.shape
    targets = o_ref.shape[0]
    slots = rows // targets
    fields = columns // 2
    loads, stores = [], []
    for f in range(fields):
        some = pl.ds(2 * f, 2)
        loads.append(pltpu.make_async_copy(x_hbm.at[some], x_ref.at[some], in_sems.at[f]))
        loads[f].start()
    wide = []
    for f in range(fields):
        loads[f].wait()
        both = jnp.concatenate([x_ref[2 * f, :WIDE, :], x_ref[2 * f + 1, :WIDE, :]], 0)
        wide.append(jnp.transpose(both))
    last = [x_ref[c, WIDE:, :] for c in range(columns)]
    rest = jnp.transpose(jnp.concatenate(last + last[:2], 0))
    chunk = targets // 4
    for t, target in enumerate(exchange_order(targets)):
        base = target * slots
        for f in range(fields):
            o_ref[t, f * slots : (f + 1) * slots, :] = wide[f][base : base + slots]
        groups = [rest[base + g * GROUP : base + (g + 1) * GROUP] for g in range(5)]
        for g in range(4):
            at = fields * slots + g * GROUP
            tile = groups[g]
            if g < fields:
                tile = jnp.concatenate([tile[:, : 6 * REST], groups[4][:, 2 * g * REST : 2 * (g + 1) * REST]], 1)
            o_ref[t, at : at + GROUP, :] = tile
        if (t + 1) % chunk == 0:
            i = t // chunk
            some = pl.ds(i * chunk, chunk)
            stores.append(pltpu.make_async_copy(o_ref.at[some], o_hbm.at[some], out_sems.at[i]))
            stores[i].start()
    for store in stores:
        store.wait()


def pack(x, targets):
    columns, degrees, rows = x.shape
    out = (targets, columns // 2 * (rows // targets) + 4 * GROUP, LANES)
    return pl.pallas_call(
        pack_kernel,
        in_specs=[pl.BlockSpec(memory_space=pl.ANY)],
        out_specs=pl.BlockSpec(memory_space=pl.ANY),
        out_shape=jax.ShapeDtypeStruct(out, x.dtype),
        scratch_shapes=[
            pltpu.VMEM(x.shape, x.dtype),
            pltpu.VMEM(out, x.dtype),
            pltpu.SemaphoreType.DMA((columns // 2,)),
            pltpu.SemaphoreType.DMA((4,)),
        ],
        compiler_params=params(56),
        cost_estimate=cost(0, 4_000_000),
        name="pack",
    )(x)


def section_kernel(copies, r_hbm, x_ref, m_ref, *rest):
    o_ref, r_ref, s_ref, f_ref, sem = rest[-5:]
    sources = r_ref.shape[0]
    slots, lats, degrees = x_ref.shape
    parts = slots // GROUP
    width = GROUP * lats
    columns = s_ref.shape[1] // (2 * GROUP)
    fields = columns // 2
    half = columns * GROUP
    order = exchange_order(sources)
    places = [order.index(e) for e in range(sources)]
    arrive = pltpu.make_async_copy(r_hbm, r_ref, sem)
    arrive.start()
    row = lax.broadcasted_iota(jnp.int32, (2 * half, width), 0)
    lane = lax.broadcasted_iota(jnp.int32, (2 * half, width), 1)
    same = (row % GROUP == lane // lats).reshape(2 * columns, GROUP, width)
    degree = lax.broadcasted_iota(jnp.int32, (GROUP, degrees), 1)
    source = lax.broadcasted_iota(jnp.int32, (width, width), 0)
    target = lax.broadcasted_iota(jnp.int32, (width, width), 1)
    move = (target == source % lats * GROUP + source // lats).astype(jnp.float32).astype(s_ref.dtype)
    masks = []
    for g in range(parts):
        wave = m_ref[g * GROUP : (g + 1) * GROUP, :]
        live = degree >= wave
        sign = (1 - 2 * ((degree + wave) % 2)).astype(jnp.float32)
        north = jnp.where(live, 1.0, 0.0).astype(s_ref.dtype)
        south = jnp.where(live, sign, 0.0).astype(s_ref.dtype)
        masks.append((north, south))
    arrive.wait()
    for g in range(parts):
        north, south = masks[g]
        for c in range(columns):
            at = c // 2 * slots + g * GROUP
            lo = c % 2 * WIDE
            tile, rest_lo = rest_place(c, g)
            rest_at = fields * slots + tile * GROUP
            pieces = []
            for e in places:
                pieces.append(r_ref[e, at : at + GROUP, lo : lo + WIDE])
                pieces.append(r_ref[e, rest_at : rest_at + GROUP, rest_lo : rest_lo + REST])
            tile = jnp.concatenate(pieces, 1)
            to = (c % 2 * 2 * fields + c // 2) * GROUP
            s_ref[g, to : to + GROUP, :] = tile * north
            to += fields * GROUP
            s_ref[g, to : to + GROUP, :] = tile * south
        basis = x_ref[g * GROUP : (g + 1) * GROUP].reshape(width, degrees)
        sums = lax.dot_general(
            s_ref[g], basis, (((1,), (1,)), ((), ())), preferred_element_type=jnp.float32
        )
        found = jnp.sum(jnp.where(same, sums.reshape(same.shape), 0.0), axis=1)
        for i in range(2):
            at, first = g * 16 + 8 * i, 2 * fields * i
            f_ref[at : at + 2 * fields, :] = found[first : first + 2 * fields]
            f_ref[at + 2 * fields : at + 2 * fields + 1, :] = found[first : first + 1]
            f_ref[at + 2 * fields + 1 : at + 8, :] = found[first + fields : first + fields + 1]
    moved = jnp.dot(f_ref[...].astype(s_ref.dtype), move, preferred_element_type=jnp.float32)
    blank = jnp.zeros((16, LANES - slots), jnp.float32)
    for l in range(lats):
        pieces = [moved[g * 16 : (g + 1) * 16, l * GROUP : (l + 1) * GROUP] for g in range(parts)]
        tile = jnp.concatenate(pieces + [blank], 1).astype(o_ref.dtype)
        for v in range(copies):
            o_ref[l, v] = tile


def section(received, legendre, waves, ready, columns, copies):
    slots, lats, degrees = legendre.shape
    parts = slots // GROUP
    spaces = [pl.ANY, pltpu.VMEM, pltpu.VMEM] + [pl.ANY] * len(ready)
    return pl.pallas_call(
        functools.partial(section_kernel, copies),
        in_specs=[pl.BlockSpec(memory_space=space) for space in spaces],
        out_specs=pl.BlockSpec(memory_space=pltpu.VMEM),
        out_shape=jax.ShapeDtypeStruct((lats, copies, 16, LANES), received.dtype),
        scratch_shapes=[
            pltpu.VMEM(received.shape, received.dtype),
            pltpu.VMEM((parts, 2 * columns * GROUP, degrees), received.dtype),
            pltpu.VMEM((parts * 16, GROUP * lats), jnp.float32),
            pltpu.SemaphoreType.DMA,
        ],
        compiler_params=params(),
        cost_estimate=cost(10_000_000_000, 4_000_000),
        name="section",
    )(received, legendre, waves, *ready)


def plain_section(received, legendre, waves, copies):
    columns, slots, degrees = received.shape
    fields = columns // 2
    degree = lax.broadcasted_iota(jnp.int32, (slots, degrees), 1)
    live = degree >= waves[:, None]
    odd = (degree + waves[:, None]) % 2 == 1
    blank = jnp.zeros_like(received)
    north = jnp.where(live[None], received, blank)
    south = jnp.where(odd[None], -north, north)
    both = jnp.stack([north, south], 0).reshape(2, fields, 2, slots, degrees)
    sums = jnp.einsum("sln,hfisn->lihfs", legendre, both, preferred_element_type=jnp.float32)
    lats = legendre.shape[1]
    rows = jnp.concatenate([sums.reshape(lats, 2, 2 * fields, slots), sums[:, :, :, 0]], 2)
    rows = rows.reshape(lats, 16, slots).astype(received.dtype)
    rows = jnp.pad(rows, ((0, 0), (0, 0), (0, LANES - slots)))
    return jnp.broadcast_to(rows[:, None], (lats, copies, 16, LANES))


def turn(product, points):
    inverse = 1.0 / points
    whole = jnp.floor(product * inverse + 0.5)
    residue = product - whole * points
    quarter = jnp.floor(4.0 * residue * inverse + 0.5)
    small = (4.0 * residue - quarter * points) * inverse * (0.5 * math.pi)
    square = small * small
    sine = small * (1.0 + square * (-1.0 / 6 + square * (1.0 / 120 + square * (-1.0 / 5040))))
    cosine = 1.0 + square * (-0.5 + square * (1.0 / 24 + square * (-1.0 / 720 + square * (1.0 / 40320))))
    which = quarter.astype(jnp.int32) & 3
    swap = (which & 1) == 1
    first = jnp.where(swap, sine, cosine)
    second = jnp.where(swap, cosine, sine)
    first = jnp.where((which == 1) | (which == 2), -first, first)
    second = jnp.where(which >= 2, -second, second)
    return first, second


def table_kernel(points_ref, m_ref, _, t_ref, c_ref, s_ref, done_ref):
    done_ref[...] = jnp.zeros_like(done_ref)
    points = points_ref[0].astype(jnp.float32)
    m = m_ref[...].astype(jnp.float32)
    down = jnp.transpose(jnp.broadcast_to(m, (LANES, LANES)))
    down = jnp.concatenate([down] * (FINE // LANES), 1)
    point = lax.broadcasted_iota(jnp.int32, (LANES, FINE), 1).astype(jnp.float32)
    cosine, sine = turn(down * point, points)
    t_ref[0] = cosine.astype(t_ref.dtype)
    t_ref[1] = (-sine).astype(t_ref.dtype)
    coarse = lax.broadcasted_iota(jnp.int32, c_ref.shape, 0) * FINE
    cosine, sine = turn(m * coarse.astype(jnp.float32), points)
    share = jnp.where(m == 0.0, 1.0, 2.0)
    c_ref[...] = cosine * share
    s_ref[...] = sine * share


def tables(points, slot_waves, early):
    depth = slot_waves.shape[1]
    steps = -(-COARSE // 8) * 8
    return pl.pallas_call(
        table_kernel,
        grid=(depth // LANES,),
        in_specs=[
            pl.BlockSpec(memory_space=pltpu.SMEM),
            pl.BlockSpec((1, LANES), lambda i: (0, i)),
            pl.BlockSpec(memory_space=pl.ANY),
        ],
        out_specs=[
            pl.BlockSpec((2, LANES, FINE), lambda i: (0, i, 0)),
            pl.BlockSpec((steps, LANES), lambda i: (0, i)),
            pl.BlockSpec((steps, LANES), lambda i: (0, i)),
            pl.BlockSpec((8, LANES), lambda i: (0, 0)),
        ],
        out_shape=[
            jax.ShapeDtypeStruct((2, depth, FINE), jnp.bfloat16),
            jax.ShapeDtypeStruct((steps, depth), jnp.float32),
            jax.ShapeDtypeStruct((steps, depth), jnp.float32),
            jax.ShapeDtypeStruct((8, LANES), jnp.float32),
        ],
        compiler_params=params(16),
        cost_estimate=cost(60_000_000, 3_000_000),
        name="tables",
    )(points, slot_waves, early)


def level_weights(scales, me, spare):
    level = jnp.arange(scales.shape[0])[:, None]
    row = jnp.arange(16)[None] % 8
    summed = jnp.where(level >= me, scales[:, None], 0.0)
    weights = jnp.where(row >= spare, summed, (level == me).astype(jnp.float32))
    return jnp.broadcast_to(weights[:, :, None], weights.shape + (LANES,))


def synth_kernel(points_ref, w_ref, r_ref, t_ref, c_ref, s_ref, v_ref, h_ref, g_ref):
    sources, levels = r_ref.shape[:2]
    depth = c_ref.shape[1]
    slots = depth // sources
    fields = v_ref.shape[1]
    pieces = []
    for e in range(sources):
        rows = sum(w_ref[v] * r_ref[e, v].astype(jnp.float32) for v in range(levels))
        pieces.append(rows[:, :slots])
    every = jnp.concatenate(pieces, 1)
    real, imag = every[:8], every[8:]
    for pair in range(g_ref.shape[0] // 16):
        first, second = [], []
        for b in (2 * pair, 2 * pair + 1):
            cosine, sine = c_ref[b : b + 1, :], s_ref[b : b + 1, :]
            first.append(real * cosine - imag * sine)
            second.append(real * sine + imag * cosine)
        to = slice(pair * 16, pair * 16 + 16)
        g_ref[to, :depth] = jnp.concatenate(first, 0).astype(g_ref.dtype)
        g_ref[to, depth:] = jnp.concatenate(second, 0).astype(g_ref.dtype)
    table = t_ref[...].reshape(2 * depth, FINE)
    values = jnp.dot(g_ref[...], table, preferred_element_type=jnp.float32)
    lane = lax.broadcasted_iota(jnp.int32, (8, FINE), 1)
    for b in range(COARSE):
        at = slice(b * FINE, (b + 1) * FINE)
        part = jnp.where(lane + b * FINE < points_ref[0], values[8 * b : 8 * b + 8], 0.0)
        for h in range(2):
            for f in range(fields):
                v_ref[h, f, :, at] = part[h * fields + f : h * fields + f + 1]
            h_ref[h, 0, :, at] = part[2 * fields + h : 2 * fields + h + 1]


def synthesis(points, weights, received, table, cosine, sine, fields):
    depth = cosine.shape[1]
    smem, vmem = pl.BlockSpec(memory_space=pltpu.SMEM), pl.BlockSpec(memory_space=pltpu.VMEM)
    return pl.pallas_call(
        synth_kernel,
        in_specs=[smem] + [vmem] * 5,
        out_specs=[vmem] * 2,
        out_shape=[
            jax.ShapeDtypeStruct((2, fields, 1, PCOL), jnp.float32),
            jax.ShapeDtypeStruct((2, 1, 1, PCOL), jnp.float32),
        ],
        scratch_shapes=[pltpu.VMEM(((COARSE + 1) // 2 * 16, 2 * depth), jnp.bfloat16)],
        compiler_params=params(),
        cost_estimate=cost(1_000_000_000, 3_000_000),
        name="synth",
    )(points, weights, received, table, cosine, sine)


def shards(spectra, legendre, slot_wavenumbers, cycle_points, layer_depth_scaling):
    slots, lats, degrees = legendre.shape
    levels_here, fields = spectra.shape[:2]
    assert levels_here == 1 and cycle_points.shape[0] == 1 and fields == 3
    waves, levels = lax.axis_size("wave"), lax.axis_size("lev")
    columns = fields * 2
    own = lax.dynamic_slice_in_dim(slot_wavenumbers, lax.axis_index("wave") * slots, slots)
    x = spectra.reshape(columns, waves * slots, spectra.shape[4])
    table, cosine, sine, done = tables(cycle_points, slot_wavenumbers[None], legendre)
    scales = lax.all_gather(layer_depth_scaling, "lev", tiled=True)
    weights = level_weights(scales, lax.axis_index("lev"), 2 * fields)
    if spectra.shape[4] == WIDE + REST and waves % 4 == 0 and fields == 3 and slots == 5 * GROUP and lats == 16:
        sent = pack(jnp.swapaxes(x, 1, 2), waves)
        order = [exchange_order(waves)]
        received = lax.all_to_all(sent, "wave", 0, 0, axis_index_groups=order, tiled=True)
        ready = (done, weights)
        rows = section(received, legendre, own[:, None], ready, columns, levels)
    else:
        received = lax.all_to_all(x, "wave", split_axis=1, concat_axis=2, tiled=True)
        rows = plain_section(received, legendre, own, levels)
    rows = rows.reshape(waves * levels, 16, LANES)
    rows = lax.all_to_all(rows, ("wave", "lev"), 0, 0, tiled=True)
    rows = rows.reshape(waves, levels, 16, LANES)
    values, height = synthesis(cycle_points, weights, rows, table, cosine, sine, fields)
    return jnp.transpose(values, (0, 2, 1, 3))[:, :, None], height


def solution(mesh):
    in_specs = (P("lev", None, None, None, "wave"), P("wave", None, None), P(), P("wave"), P("lev"))
    out_specs = (P(None, "wave", "lev", None, None), P(None, "wave", "lev", None))
    call = jax.shard_map(shards, mesh=mesh, in_specs=in_specs, out_specs=out_specs, check_vma=False)

    def whole(*arrays):
        values, height = call(*arrays)
        return values, height

    return whole
```

```python
import functools
import math

import jax
import jax.numpy as jnp
from jax import lax
from jax.experimental import pallas as pl
from jax.experimental.pallas import tpu as pltpu
from jax.sharding import PartitionSpec as P

PCOL = 5376
LANES = 128
FINE = 256
COARSE = PCOL // FINE
GROUP = 16
WIDE = 64
REST = 16


def cost(flops, size):
    return pl.CostEstimate(flops=flops, bytes_accessed=size, transcendentals=0)


def params(size=16):
    return pltpu.CompilerParams(vmem_limit_bytes=size * 1024 * 1024)


def exchange_order(devices):
    if devices == 16:
        return [10, 7, 6, 14, 2, 0, 13, 15, 12, 9, 11, 5, 3, 4, 8, 1]
    return list(range(devices))


def rest_place(c, g):
    return (g, c * REST) if g < 4 else (c // 2, (6 + c % 2) * REST)


def pack_kernel(x_hbm, o_hbm, x_ref, o_ref, in_sems, out_sems):
    columns, _, rows = x_ref.shape
    targets = o_ref.shape[0]
    slots = rows // targets
    fields = columns // 2
    loads, stores = [], []
    for f in range(fields):
        some = pl.ds(2 * f, 2)
        loads.append(pltpu.make_async_copy(x_hbm.at[some], x_ref.at[some], in_sems.at[f]))
        loads[f].start()
    wide = []
    for f in range(fields):
        loads[f].wait()
        both = jnp.concatenate([x_ref[2 * f, :WIDE, :], x_ref[2 * f + 1, :WIDE, :]], 0)
        wide.append(jnp.transpose(both))
    last = [x_ref[c, WIDE:, :] for c in range(columns)]
    rest = jnp.transpose(jnp.concatenate(last + last[:2], 0))
    chunk = targets // 4
    for t, target in enumerate(exchange_order(targets)):
        base = target * slots
        for f in range(fields):
            o_ref[t, f * slots : (f + 1) * slots, :] = wide[f][base : base + slots]
        groups = [rest[base + g * GROUP : base + (g + 1) * GROUP] for g in range(5)]
        for g in range(4):
            at = fields * slots + g * GROUP
            tile = groups[g]
            if g < fields:
                tile = jnp.concatenate([tile[:, : 6 * REST], groups[4][:, 2 * g * REST : 2 * (g + 1) * REST]], 1)
            o_ref[t, at : at + GROUP, :] = tile
        if (t + 1) % chunk == 0:
            i = t // chunk
            some = pl.ds(i * chunk, chunk)
            stores.append(pltpu.make_async_copy(o_ref.at[some], o_hbm.at[some], out_sems.at[i]))
            stores[i].start()
    for store in stores:
        store.wait()


def pack(x, targets):
    columns, degrees, rows = x.shape
    out = (targets, columns // 2 * (rows // targets) + 4 * GROUP, LANES)
    return pl.pallas_call(
        pack_kernel,
        in_specs=[pl.BlockSpec(memory_space=pl.ANY)],
        out_specs=pl.BlockSpec(memory_space=pl.ANY),
        out_shape=jax.ShapeDtypeStruct(out, x.dtype),
        scratch_shapes=[
            pltpu.VMEM(x.shape, x.dtype),
            pltpu.VMEM(out, x.dtype),
            pltpu.SemaphoreType.DMA((columns // 2,)),
            pltpu.SemaphoreType.DMA((4,)),
        ],
        compiler_params=params(56),
        cost_estimate=cost(0, 4_000_000),
        name="pack",
    )(x)


def section_kernel(copies, r_hbm, x_ref, m_ref, *rest):
    o_ref, r_ref, s_ref, f_ref, sem = rest[-5:]
    sources = r_ref.shape[0]
    slots, lats, degrees = x_ref.shape
    parts = slots // GROUP
    width = GROUP * lats
    columns = s_ref.shape[1] // (2 * GROUP)
    fields = columns // 2
    half = columns * GROUP
    order = exchange_order(sources)
    places = [order.index(e) for e in range(sources)]
    arrive = pltpu.make_async_copy(r_hbm, r_ref, sem)
    arrive.start()
    row = lax.broadcasted_iota(jnp.int32, (2 * half, width), 0)
    lane = lax.broadcasted_iota(jnp.int32, (2 * half, width), 1)
    same = (row % GROUP == lane // lats).reshape(2 * columns, GROUP, width)
    degree = lax.broadcasted_iota(jnp.int32, (GROUP, degrees), 1)
    source = lax.broadcasted_iota(jnp.int32, (width, width), 0)
    target = lax.broadcasted_iota(jnp.int32, (width, width), 1)
    move = (target == source % lats * GROUP + source // lats).astype(jnp.float32).astype(s_ref.dtype)
    masks = []
    for g in range(parts):
        wave = m_ref[g * GROUP : (g + 1) * GROUP, :]
        live = degree >= wave
        sign = (1 - 2 * ((degree + wave) % 2)).astype(jnp.float32)
        north = jnp.where(live, 1.0, 0.0).astype(s_ref.dtype)
        south = jnp.where(live, sign, 0.0).astype(s_ref.dtype)
        masks.append((north, south))
    arrive.wait()
    for g in range(parts):
        north, south = masks[g]
        for c in range(columns):
            at = c // 2 * slots + g * GROUP
            lo = c % 2 * WIDE
            tile, rest_lo = rest_place(c, g)
            rest_at = fields * slots + tile * GROUP
            pieces = []
            for e in places:
                pieces.append(r_ref[e, at : at + GROUP, lo : lo + WIDE])
                pieces.append(r_ref[e, rest_at : rest_at + GROUP, rest_lo : rest_lo + REST])
            tile = jnp.concatenate(pieces, 1)
            to = (c % 2 * 2 * fields + c // 2) * GROUP
            s_ref[g, to : to + GROUP, :] = tile * north
            to += fields * GROUP
            s_ref[g, to : to + GROUP, :] = tile * south
        basis = x_ref[g * GROUP : (g + 1) * GROUP].reshape(width, degrees)
        sums = lax.dot_general(
            s_ref[g], basis, (((1,), (1,)), ((), ())), preferred_element_type=jnp.float32
        )
        found = jnp.sum(jnp.where(same, sums.reshape(same.shape), 0.0), axis=1)
        for i in range(2):
            at, first = g * 16 + 8 * i, 2 * fields * i
            f_ref[at : at + 2 * fields, :] = found[first : first + 2 * fields]
            f_ref[at + 2 * fields : at + 2 * fields + 1, :] = found[first : first + 1]
            f_ref[at + 2 * fields + 1 : at + 8, :] = found[first + fields : first + fields + 1]
    moved = jnp.dot(f_ref[...].astype(s_ref.dtype), move, preferred_element_type=jnp.float32)
    blank = jnp.zeros((16, LANES - slots), jnp.float32)
    for l in range(lats):
        pieces = [moved[g * 16 : (g + 1) * 16, l * GROUP : (l + 1) * GROUP] for g in range(parts)]
        tile = jnp.concatenate(pieces + [blank], 1).astype(o_ref.dtype)
        for v in range(copies):
            o_ref[l, v] = tile


def section(received, legendre, waves, ready, columns, copies):
    slots, lats, degrees = legendre.shape
    parts = slots // GROUP
    spaces = [pl.ANY, pltpu.VMEM, pltpu.VMEM] + [pl.ANY] * len(ready)
    return pl.pallas_call(
        functools.partial(section_kernel, copies),
        in_specs=[pl.BlockSpec(memory_space=space) for space in spaces],
        out_specs=pl.BlockSpec(memory_space=pltpu.VMEM),
        out_shape=jax.ShapeDtypeStruct((lats, copies, 16, LANES), received.dtype),
        scratch_shapes=[
            pltpu.VMEM(received.shape, received.dtype),
            pltpu.VMEM((parts, 2 * columns * GROUP, degrees), received.dtype),
            pltpu.VMEM((parts * 16, GROUP * lats), jnp.float32),
            pltpu.SemaphoreType.DMA,
        ],
        compiler_params=params(),
        cost_estimate=cost(10_000_000_000, 4_000_000),
        name="section",
    )(received, legendre, waves, *ready)


def plain_section(received, legendre, waves, copies):
    columns, slots, degrees = received.shape
    fields = columns // 2
    degree = lax.broadcasted_iota(jnp.int32, (slots, degrees), 1)
    live = degree >= waves[:, None]
    odd = (degree + waves[:, None]) % 2 == 1
    blank = jnp.zeros_like(received)
    north = jnp.where(live[None], received, blank)
    south = jnp.where(odd[None], -north, north)
    both = jnp.stack([north, south], 0).reshape(2, fields, 2, slots, degrees)
    sums = jnp.einsum("sln,hfisn->lihfs", legendre, both, preferred_element_type=jnp.float32)
    lats = legendre.shape[1]
    rows = jnp.concatenate([sums.reshape(lats, 2, 2 * fields, slots), sums[:, :, :, 0]], 2)
    rows = rows.reshape(lats, 16, slots).astype(received.dtype)
    rows = jnp.pad(rows, ((0, 0), (0, 0), (0, LANES - slots)))
    return jnp.broadcast_to(rows[:, None], (lats, copies, 16, LANES))


def turn(product, points):
    inverse = 1.0 / points
    whole = jnp.floor(product * inverse + 0.5)
    residue = product - whole * points
    quarter = jnp.floor(4.0 * residue * inverse + 0.5)
    small = (4.0 * residue - quarter * points) * inverse * (0.5 * math.pi)
    square = small * small
    sine = small * (1.0 + square * (-1.0 / 6 + square * (1.0 / 120 + square * (-1.0 / 5040))))
    cosine = 1.0 + square * (-0.5 + square * (1.0 / 24 + square * (-1.0 / 720 + square * (1.0 / 40320))))
    which = quarter.astype(jnp.int32) & 3
    swap = (which & 1) == 1
    first = jnp.where(swap, sine, cosine)
    second = jnp.where(swap, cosine, sine)
    first = jnp.where((which == 1) | (which == 2), -first, first)
    second = jnp.where(which >= 2, -second, second)
    return first, second


def table_kernel(points_ref, m_ref, _, t_ref, c_ref, s_ref, done_ref):
    done_ref[...] = jnp.zeros_like(done_ref)
    points = points_ref[0].astype(jnp.float32)
    m = m_ref[...].astype(jnp.float32)
    down = jnp.transpose(jnp.broadcast_to(m, (LANES, LANES)))
    down = jnp.concatenate([down] * (FINE // LANES), 1)
    point = lax.broadcasted_iota(jnp.int32, (LANES, FINE), 1).astype(jnp.float32)
    cosine, sine = turn(down * point, points)
    t_ref[0] = cosine.astype(t_ref.dtype)
    t_ref[1] = (-sine).astype(t_ref.dtype)
    coarse = lax.broadcasted_iota(jnp.int32, c_ref.shape, 0) * FINE
    cosine, sine = turn(m * coarse.astype(jnp.float32), points)
    share = jnp.where(m == 0.0, 1.0, 2.0)
    c_ref[...] = cosine * share
    s_ref[...] = sine * share


def tables(points, slot_waves, early):
    depth = slot_waves.shape[1]
    steps = -(-COARSE // 8) * 8
    return pl.pallas_call(
        table_kernel,
        grid=(depth // LANES,),
        in_specs=[
            pl.BlockSpec(memory_space=pltpu.SMEM),
            pl.BlockSpec((1, LANES), lambda i: (0, i)),
            pl.BlockSpec(memory_space=pl.ANY),
        ],
        out_specs=[
            pl.BlockSpec((2, LANES, FINE), lambda i: (0, i, 0)),
            pl.BlockSpec((steps, LANES), lambda i: (0, i)),
            pl.BlockSpec((steps, LANES), lambda i: (0, i)),
            pl.BlockSpec((8, LANES), lambda i: (0, 0)),
        ],
        out_shape=[
            jax.ShapeDtypeStruct((2, depth, FINE), jnp.bfloat16),
            jax.ShapeDtypeStruct((steps, depth), jnp.float32),
            jax.ShapeDtypeStruct((steps, depth), jnp.float32),
            jax.ShapeDtypeStruct((8, LANES), jnp.float32),
        ],
        compiler_params=params(16),
        cost_estimate=cost(60_000_000, 3_000_000),
        name="tables",
    )(points, slot_waves, early)


def level_weights(scales, me, spare):
    level = jnp.arange(scales.shape[0])[:, None]
    row = jnp.arange(16)[None] % 8
    summed = jnp.where(level >= me, scales[:, None], 0.0)
    weights = jnp.where(row >= spare, summed, (level == me).astype(jnp.float32))
    return jnp.broadcast_to(weights[:, :, None], weights.shape + (LANES,))


def synth_kernel(points_ref, w_ref, r_ref, t_ref, c_ref, s_ref, v_ref, h_ref, g_ref):
    sources, levels = r_ref.shape[:2]
    depth = c_ref.shape[1]
    slots = depth // sources
    fields = v_ref.shape[1]
    pieces = []
    for e in range(sources):
        rows = sum(w_ref[v] * r_ref[e, v].astype(jnp.float32) for v in range(levels))
        pieces.append(rows[:, :slots])
    every = jnp.concatenate(pieces, 1)
    real, imag = every[:8], every[8:]
    for pair in range(g_ref.shape[0] // 16):
        first, second = [], []
        for b in (2 * pair, 2 * pair + 1):
            cosine, sine = c_ref[b : b + 1, :], s_ref[b : b + 1, :]
            first.append(real * cosine - imag * sine)
            second.append(real * sine + imag * cosine)
        to = slice(pair * 16, pair * 16 + 16)
        g_ref[to, :depth] = jnp.concatenate(first, 0).astype(g_ref.dtype)
        g_ref[to, depth:] = jnp.concatenate(second, 0).astype(g_ref.dtype)
    table = t_ref[...].reshape(2 * depth, FINE)
    values = jnp.dot(g_ref[...], table, preferred_element_type=jnp.float32)
    lane = lax.broadcasted_iota(jnp.int32, (8, FINE), 1)
    for b in range(COARSE):
        at = slice(b * FINE, (b + 1) * FINE)
        part = jnp.where(lane + b * FINE < points_ref[0], values[8 * b : 8 * b + 8], 0.0)
        for h in range(2):
            for f in range(fields):
                v_ref[h, f, :, at] = part[h * fields + f : h * fields + f + 1]
            h_ref[h, 0, :, at] = part[2 * fields + h : 2 * fields + h + 1]


def synthesis(points, weights, received, table, cosine, sine, fields):
    depth = cosine.shape[1]
    smem, vmem = pl.BlockSpec(memory_space=pltpu.SMEM), pl.BlockSpec(memory_space=pltpu.VMEM)
    return pl.pallas_call(
        synth_kernel,
        in_specs=[smem] + [vmem] * 5,
        out_specs=[vmem] * 2,
        out_shape=[
            jax.ShapeDtypeStruct((2, fields, 1, PCOL), jnp.float32),
            jax.ShapeDtypeStruct((2, 1, 1, PCOL), jnp.float32),
        ],
        scratch_shapes=[pltpu.VMEM(((COARSE + 1) // 2 * 16, 2 * depth), jnp.bfloat16)],
        compiler_params=params(),
        cost_estimate=cost(1_000_000_000, 3_000_000),
        name="synth",
    )(points, weights, received, table, cosine, sine)


def shards(spectra, legendre, slot_wavenumbers, cycle_points, layer_depth_scaling):
    slots, lats, degrees = legendre.shape
    levels_here, fields = spectra.shape[:2]
    assert levels_here == 1 and cycle_points.shape[0] == 1 and fields == 3
    waves, levels = lax.axis_size("wave"), lax.axis_size("lev")
    columns = fields * 2
    own = lax.dynamic_slice_in_dim(slot_wavenumbers, lax.axis_index("wave") * slots, slots)
    x = spectra.reshape(columns, waves * slots, spectra.shape[4])
    table, cosine, sine, done = tables(cycle_points, slot_wavenumbers[None], legendre)
    scales = lax.all_gather(layer_depth_scaling, "lev", tiled=True)
    weights = level_weights(scales, lax.axis_index("lev"), 2 * fields)
    if spectra.shape[4] == WIDE + REST and waves % 4 == 0 and fields == 3 and slots == 5 * GROUP and lats == 16:
        sent = pack(jnp.swapaxes(x, 1, 2), waves)
        order = [exchange_order(waves)]
        received = lax.all_to_all(sent, "wave", 0, 0, axis_index_groups=order, tiled=True)
        ready = (done, weights)
        rows = section(received, legendre, own[:, None], ready, columns, levels)
    else:
        received = lax.all_to_all(x, "wave", split_axis=1, concat_axis=2, tiled=True)
        rows = plain_section(received, legendre, own, levels)
    rows = rows.reshape(waves * levels, 16, LANES)
    rows = lax.all_to_all(rows, ("wave", "lev"), 0, 0, tiled=True)
    rows = rows.reshape(waves, levels, 16, LANES)
    values, height = synthesis(cycle_points, weights, rows, table, cosine, sine, fields)
    return jnp.transpose(values, (0, 2, 1, 3))[:, :, None], height


def solution(mesh):
    in_specs = (P("lev", None, None, None, "wave"), P("wave", None, None), P(), P("wave"), P("lev"))
    out_specs = (P(None, "wave", "lev", None, None), P(None, "wave", "lev", None))
    call = jax.shard_map(shards, mesh=mesh, in_specs=in_specs, out_specs=out_specs, check_vma=False)

    def whole(*arrays):
        values, height = call(*arrays)
        return values, height

    return whole
```

```python
import functools
import math

import jax
import jax.numpy as jnp
from jax import lax
from jax.experimental import pallas as pl
from jax.experimental.pallas import tpu as pltpu
from jax.sharding import PartitionSpec as P

PCOL = 5376
LANES = 128
FINE = 256
COARSE = PCOL // FINE
GROUP = 16
WIDE = 64
REST = 16


def cost(flops, size):
    return pl.CostEstimate(flops=flops, bytes_accessed=size, transcendentals=0)


def params(size=16):
    return pltpu.CompilerParams(vmem_limit_bytes=size * 1024 * 1024)


def exchange_order(devices):
    bits = (devices - 1).bit_length()
    return sorted(range(devices), key=lambda i: -int(format(i, "0" + str(bits) + "b")[::-1], 2))


def rest_place(c, g):
    return (g, c * REST) if g < 4 else (c // 2, (6 + c % 2) * REST)


def pack_kernel(x_hbm, o_hbm, x_ref, o_ref, in_sems, out_sems):
    columns, _, rows = x_ref.shape
    targets = o_ref.shape[0]
    slots = rows // targets
    fields = columns // 2
    loads, stores = [], []
    for f in range(fields):
        some = pl.ds(2 * f, 2)
        loads.append(pltpu.make_async_copy(x_hbm.at[some], x_ref.at[some], in_sems.at[f]))
        loads[f].start()
    wide = []
    for f in range(fields):
        loads[f].wait()
        both = jnp.concatenate([x_ref[2 * f, :WIDE, :], x_ref[2 * f + 1, :WIDE, :]], 0)
        wide.append(jnp.transpose(both))
    last = [x_ref[c, WIDE:, :] for c in range(columns)]
    rest = jnp.transpose(jnp.concatenate(last + last[:2], 0))
    chunk = targets // 4
    for t, target in enumerate(exchange_order(targets)):
        base = target * slots
        for f in range(fields):
            o_ref[t, f * slots : (f + 1) * slots, :] = wide[f][base : base + slots]
        groups = [rest[base + g * GROUP : base + (g + 1) * GROUP] for g in range(5)]
        for g in range(4):
            at = fields * slots + g * GROUP
            tile = groups[g]
            if g < fields:
                tile = jnp.concatenate([tile[:, : 6 * REST], groups[4][:, 2 * g * REST : 2 * (g + 1) * REST]], 1)
            o_ref[t, at : at + GROUP, :] = tile
        if (t + 1) % chunk == 0:
            i = t // chunk
            some = pl.ds(i * chunk, chunk)
            stores.append(pltpu.make_async_copy(o_ref.at[some], o_hbm.at[some], out_sems.at[i]))
            stores[i].start()
    for store in stores:
        store.wait()


def pack(x, targets):
    columns, degrees, rows = x.shape
    out = (targets, columns // 2 * (rows // targets) + 4 * GROUP, LANES)
    return pl.pallas_call(
        pack_kernel,
        in_specs=[pl.BlockSpec(memory_space=pl.ANY)],
        out_specs=pl.BlockSpec(memory_space=pl.ANY),
        out_shape=jax.ShapeDtypeStruct(out, x.dtype),
        scratch_shapes=[
            pltpu.VMEM(x.shape, x.dtype),
            pltpu.VMEM(out, x.dtype),
            pltpu.SemaphoreType.DMA((columns // 2,)),
            pltpu.SemaphoreType.DMA((4,)),
        ],
        compiler_params=params(56),
        cost_estimate=cost(0, 4_000_000),
        name="pack",
    )(x)


def section_kernel(copies, r_hbm, x_ref, m_ref, *rest):
    o_ref, r_ref, s_ref, f_ref, sem = rest[-5:]
    sources = r_ref.shape[0]
    slots, lats, degrees = x_ref.shape
    parts = slots // GROUP
    width = GROUP * lats
    columns = s_ref.shape[1] // (2 * GROUP)
    fields = columns // 2
    half = columns * GROUP
    order = exchange_order(sources)
    places = [order.index(e) for e in range(sources)]
    arrive = pltpu.make_async_copy(r_hbm, r_ref, sem)
    arrive.start()
    row = lax.broadcasted_iota(jnp.int32, (2 * half, width), 0)
    lane = lax.broadcasted_iota(jnp.int32, (2 * half, width), 1)
    same = (row % GROUP == lane // lats).reshape(2 * columns, GROUP, width)
    degree = lax.broadcasted_iota(jnp.int32, (GROUP, degrees), 1)
    source = lax.broadcasted_iota(jnp.int32, (width, width), 0)
    target = lax.broadcasted_iota(jnp.int32, (width, width), 1)
    move = (target == source % lats * GROUP + source // lats).astype(jnp.float32).astype(s_ref.dtype)
    masks = []
    for g in range(parts):
        wave = m_ref[g * GROUP : (g + 1) * GROUP, :]
        live = degree >= wave
        sign = (1 - 2 * ((degree + wave) % 2)).astype(jnp.float32)
        north = jnp.where(live, 1.0, 0.0).astype(s_ref.dtype)
        south = jnp.where(live, sign, 0.0).astype(s_ref.dtype)
        masks.append((north, south))
    arrive.wait()
    for g in range(parts):
        north, south = masks[g]
        for c in range(columns):
            at = c // 2 * slots + g * GROUP
            lo = c % 2 * WIDE
            tile, rest_lo = rest_place(c, g)
            rest_at = fields * slots + tile * GROUP
            pieces = []
            for e in places:
                pieces.append(r_ref[e, at : at + GROUP, lo : lo + WIDE])
                pieces.append(r_ref[e, rest_at : rest_at + GROUP, rest_lo : rest_lo + REST])
            tile = jnp.concatenate(pieces, 1)
            to = (c % 2 * 2 * fields + c // 2) * GROUP
            s_ref[g, to : to + GROUP, :] = tile * north
            to += fields * GROUP
            s_ref[g, to : to + GROUP, :] = tile * south
        basis = x_ref[g * GROUP : (g + 1) * GROUP].reshape(width, degrees)
        sums = lax.dot_general(
            s_ref[g], basis, (((1,), (1,)), ((), ())), preferred_element_type=jnp.float32
        )
        found = jnp.sum(jnp.where(same, sums.reshape(same.shape), 0.0), axis=1)
        for i in range(2):
            at, first = g * 16 + 8 * i, 2 * fields * i
            f_ref[at : at + 2 * fields, :] = found[first : first + 2 * fields]
            f_ref[at + 2 * fields : at + 2 * fields + 1, :] = found[first : first + 1]
            f_ref[at + 2 * fields + 1 : at + 8, :] = found[first + fields : first + fields + 1]
    moved = jnp.dot(f_ref[...].astype(s_ref.dtype), move, preferred_element_type=jnp.float32)
    blank = jnp.zeros((16, LANES - slots), jnp.float32)
    for l in range(lats):
        pieces = [moved[g * 16 : (g + 1) * 16, l * GROUP : (l + 1) * GROUP] for g in range(parts)]
        tile = jnp.concatenate(pieces + [blank], 1).astype(o_ref.dtype)
        for v in range(copies):
            o_ref[l, v] = tile


def section(received, legendre, waves, ready, columns, copies):
    slots, lats, degrees = legendre.shape
    parts = slots // GROUP
    spaces = [pl.ANY, pltpu.VMEM, pltpu.VMEM] + [pl.ANY] * len(ready)
    return pl.pallas_call(
        functools.partial(section_kernel, copies),
        in_specs=[pl.BlockSpec(memory_space=space) for space in spaces],
        out_specs=pl.BlockSpec(memory_space=pltpu.VMEM),
        out_shape=jax.ShapeDtypeStruct((lats, copies, 16, LANES), received.dtype),
        scratch_shapes=[
            pltpu.VMEM(received.shape, received.dtype),
            pltpu.VMEM((parts, 2 * columns * GROUP, degrees), received.dtype),
            pltpu.VMEM((parts * 16, GROUP * lats), jnp.float32),
            pltpu.SemaphoreType.DMA,
        ],
        compiler_params=params(),
        cost_estimate=cost(10_000_000_000, 4_000_000),
        name="section",
    )(received, legendre, waves, *ready)


def plain_section(received, legendre, waves, copies):
    columns, slots, degrees = received.shape
    fields = columns // 2
    degree = lax.broadcasted_iota(jnp.int32, (slots, degrees), 1)
    live = degree >= waves[:, None]
    odd = (degree + waves[:, None]) % 2 == 1
    blank = jnp.zeros_like(received)
    north = jnp.where(live[None], received, blank)
    south = jnp.where(odd[None], -north, north)
    both = jnp.stack([north, south], 0).reshape(2, fields, 2, slots, degrees)
    sums = jnp.einsum("sln,hfisn->lihfs", legendre, both, preferred_element_type=jnp.float32)
    lats = legendre.shape[1]
    rows = jnp.concatenate([sums.reshape(lats, 2, 2 * fields, slots), sums[:, :, :, 0]], 2)
    rows = rows.reshape(lats, 16, slots).astype(received.dtype)
    rows = jnp.pad(rows, ((0, 0), (0, 0), (0, LANES - slots)))
    return jnp.broadcast_to(rows[:, None], (lats, copies, 16, LANES))


def turn(product, points):
    inverse = 1.0 / points
    whole = jnp.floor(product * inverse + 0.5)
    residue = product - whole * points
    quarter = jnp.floor(4.0 * residue * inverse + 0.5)
    small = (4.0 * residue - quarter * points) * inverse * (0.5 * math.pi)
    square = small * small
    sine = small * (1.0 + square * (-1.0 / 6 + square * (1.0 / 120 + square * (-1.0 / 5040))))
    cosine = 1.0 + square * (-0.5 + square * (1.0 / 24 + square * (-1.0 / 720 + square * (1.0 / 40320))))
    which = quarter.astype(jnp.int32) & 3
    swap = (which & 1) == 1
    first = jnp.where(swap, sine, cosine)
    second = jnp.where(swap, cosine, sine)
    first = jnp.where((which == 1) | (which == 2), -first, first)
    second = jnp.where(which >= 2, -second, second)
    return first, second


def table_kernel(points_ref, m_ref, _, t_ref, c_ref, s_ref, done_ref):
    done_ref[...] = jnp.zeros_like(done_ref)
    points = points_ref[0].astype(jnp.float32)
    m = m_ref[...].astype(jnp.float32)
    down = jnp.transpose(jnp.broadcast_to(m, (LANES, LANES)))
    down = jnp.concatenate([down] * (FINE // LANES), 1)
    point = lax.broadcasted_iota(jnp.int32, (LANES, FINE), 1).astype(jnp.float32)
    cosine, sine = turn(down * point, points)
    t_ref[0] = cosine.astype(t_ref.dtype)
    t_ref[1] = (-sine).astype(t_ref.dtype)
    coarse = lax.broadcasted_iota(jnp.int32, c_ref.shape, 0) * FINE
    cosine, sine = turn(m * coarse.astype(jnp.float32), points)
    share = jnp.where(m == 0.0, 1.0, 2.0)
    c_ref[...] = cosine * share
    s_ref[...] = sine * share


def tables(points, slot_waves, early):
    depth = slot_waves.shape[1]
    steps = -(-COARSE // 8) * 8
    return pl.pallas_call(
        table_kernel,
        grid=(depth // LANES,),
        in_specs=[
            pl.BlockSpec(memory_space=pltpu.SMEM),
            pl.BlockSpec((1, LANES), lambda i: (0, i)),
            pl.BlockSpec(memory_space=pl.ANY),
        ],
        out_specs=[
            pl.BlockSpec((2, LANES, FINE), lambda i: (0, i, 0)),
            pl.BlockSpec((steps, LANES), lambda i: (0, i)),
            pl.BlockSpec((steps, LANES), lambda i: (0, i)),
            pl.BlockSpec((8, LANES), lambda i: (0, 0)),
        ],
        out_shape=[
            jax.ShapeDtypeStruct((2, depth, FINE), jnp.bfloat16),
            jax.ShapeDtypeStruct((steps, depth), jnp.float32),
            jax.ShapeDtypeStruct((steps, depth), jnp.float32),
            jax.ShapeDtypeStruct((8, LANES), jnp.float32),
        ],
        compiler_params=params(16),
        cost_estimate=cost(60_000_000, 3_000_000),
        name="tables",
    )(points, slot_waves, early)


def level_weights(scales, me, spare):
    level = jnp.arange(scales.shape[0])[:, None]
    row = jnp.arange(16)[None] % 8
    summed = jnp.where(level >= me, scales[:, None], 0.0)
    weights = jnp.where(row >= spare, summed, (level == me).astype(jnp.float32))
    return jnp.broadcast_to(weights[:, :, None], weights.shape + (LANES,))


def synth_kernel(points_ref, w_ref, r_ref, t_ref, c_ref, s_ref, v_ref, h_ref, g_ref):
    sources, levels = r_ref.shape[:2]
    depth = c_ref.shape[1]
    slots = depth // sources
    fields = v_ref.shape[1]
    pieces = []
    for e in range(sources):
        rows = sum(w_ref[v] * r_ref[e, v].astype(jnp.float32) for v in range(levels))
        pieces.append(rows[:, :slots])
    every = jnp.concatenate(pieces, 1)
    real, imag = every[:8], every[8:]
    for pair in range(g_ref.shape[0] // 16):
        first, second = [], []
        for b in (2 * pair, 2 * pair + 1):
            cosine, sine = c_ref[b : b + 1, :], s_ref[b : b + 1, :]
            first.append(real * cosine - imag * sine)
            second.append(real * sine + imag * cosine)
        to = slice(pair * 16, pair * 16 + 16)
        g_ref[to, :depth] = jnp.concatenate(first, 0).astype(g_ref.dtype)
        g_ref[to, depth:] = jnp.concatenate(second, 0).astype(g_ref.dtype)
    table = t_ref[...].reshape(2 * depth, FINE)
    values = jnp.dot(g_ref[...], table, preferred_element_type=jnp.float32)
    lane = lax.broadcasted_iota(jnp.int32, (8, FINE), 1)
    for b in range(COARSE):
        at = slice(b * FINE, (b + 1) * FINE)
        part = jnp.where(lane + b * FINE < points_ref[0], values[8 * b : 8 * b + 8], 0.0)
        for h in range(2):
            for f in range(fields):
                v_ref[h, f, :, at] = part[h * fields + f : h * fields + f + 1]
            h_ref[h, 0, :, at] = part[2 * fields + h : 2 * fields + h + 1]


def synthesis(points, weights, received, table, cosine, sine, fields):
    depth = cosine.shape[1]
    smem, vmem = pl.BlockSpec(memory_space=pltpu.SMEM), pl.BlockSpec(memory_space=pltpu.VMEM)
    return pl.pallas_call(
        synth_kernel,
        in_specs=[smem] + [vmem] * 5,
        out_specs=[vmem] * 2,
        out_shape=[
            jax.ShapeDtypeStruct((2, fields, 1, PCOL), jnp.float32),
            jax.ShapeDtypeStruct((2, 1, 1, PCOL), jnp.float32),
        ],
        scratch_shapes=[pltpu.VMEM(((COARSE + 1) // 2 * 16, 2 * depth), jnp.bfloat16)],
        compiler_params=params(),
        cost_estimate=cost(1_000_000_000, 3_000_000),
        name="synth",
    )(points, weights, received, table, cosine, sine)


def shards(spectra, legendre, slot_wavenumbers, cycle_points, layer_depth_scaling):
    slots, lats, degrees = legendre.shape
    levels_here, fields = spectra.shape[:2]
    assert levels_here == 1 and cycle_points.shape[0] == 1 and fields == 3
    waves, levels = lax.axis_size("wave"), lax.axis_size("lev")
    columns = fields * 2
    own = lax.dynamic_slice_in_dim(slot_wavenumbers, lax.axis_index("wave") * slots, slots)
    x = spectra.reshape(columns, waves * slots, spectra.shape[4])
    table, cosine, sine, done = tables(cycle_points, slot_wavenumbers[None], legendre)
    scales = lax.all_gather(layer_depth_scaling, "lev", tiled=True)
    weights = level_weights(scales, lax.axis_index("lev"), 2 * fields)
    if spectra.shape[4] == WIDE + REST and waves % 4 == 0 and fields == 3 and slots == 5 * GROUP and lats == 16:
        sent = pack(jnp.swapaxes(x, 1, 2), waves)
        order = [exchange_order(waves)]
        received = lax.all_to_all(sent, "wave", 0, 0, axis_index_groups=order, tiled=True)
        ready = (done, weights)
        rows = section(received, legendre, own[:, None], ready, columns, levels)
    else:
        received = lax.all_to_all(x, "wave", split_axis=1, concat_axis=2, tiled=True)
        rows = plain_section(received, legendre, own, levels)
    rows = rows.reshape(waves * levels, 16, LANES)
    rows = lax.all_to_all(rows, ("wave", "lev"), 0, 0, tiled=True)
    rows = rows.reshape(waves, levels, 16, LANES)
    values, height = synthesis(cycle_points, weights, rows, table, cosine, sine, fields)
    return jnp.transpose(values, (0, 2, 1, 3))[:, :, None], height


def solution(mesh):
    in_specs = (P("lev", None, None, None, "wave"), P("wave", None, None), P(), P("wave"), P("lev"))
    out_specs = (P(None, "wave", "lev", None, None), P(None, "wave", "lev", None))
    call = jax.shard_map(shards, mesh=mesh, in_specs=in_specs, out_specs=out_specs, check_vma=False)

    def whole(*arrays):
        values, height = call(*arrays)
        return values, height

    return whole
```
